32 devices in a mesh: cable: 2 (over y), blk: 4 (over z), sub: 4 (over x, core).
Axes of the slice: x: 2, y: 2, z: 4, core: 2. Of those that a mesh axis runs over, the one named last changes fastest.
Arguments:
- raw: bfloat16 [8, 8, 4096], P('cable', 'sub', 'blk'), parts along dimension 0, may hold values from -2500 to 2500
- valid: int32 [8, 8], P(('cable', 'blk'), 'sub'), parts along dimension 0, may hold values 0 or 1
- select: int32 [8, 4, 4], P(('cable', 'blk')), parts along dimension 0, may hold values 0 or 1
Outputs:
- corr: float32 [64, 4, 8, 512], P(('cable', 'blk'), None, 'sub'), parts along dimension 0
The draws below stay inside these ranges and needn't reach their ends.
There are 2 independent parts, one for each index of `cable`. The reference program is written for one: setup_inputs(seed, part) draws one part's arguments, and reference() takes and returns one part's arrays. A program takes and returns all parts, laid end to end along the dimension named above; each array names one. Nothing has to cross between parts.
All inputs are finite; a program needn't handle non-finite values. No bound on the sum of `valid` or of `select` on one device may be relied on, other than what follows from the above.
Results may differ from the reference program's by a relative error of at most 0.0023.
Values may be sent and summed in bfloat16 or wider, within the bound.
A program may use at most 128 MiB of HBM per device.

```python
import math
import jax
import jax.numpy as jnp
from jax import lax

SEG_LEN = 1024
BAND = 64
LAGS = 512
CB = 8
C = 32
SAMPLES = 4096
SEG = 4
N_BLK = 4


def draw_raw(key, part):
    key = jax.random.fold_in(key, 11)
    keys = jax.random.split(key, 7)
    chan = jnp.arange(C, dtype=jnp.int32)[:, None]
    times = jnp.arange(SAMPLES, dtype=jnp.int32)[None, :]
    noise = jnp.clip(jax.random.normal(keys[0], (C, SAMPLES), jnp.float32), -6.0, 6.0)
    gain = jnp.exp(jax.random.uniform(keys[1], (C, 1), jnp.float32, 0.0, math.log(10.0)))
    envelope = jnp.exp(jax.random.uniform(keys[2], (C, SAMPLES // 64), jnp.float32, math.log(0.3), math.log(3.0)))
    envelope = jnp.repeat(envelope, 64, axis=1)
    common = jnp.clip(jax.random.normal(keys[3], (SAMPLES,), jnp.float32), -6.0, 6.0)
    wave = 1.5 * jnp.take(common, (times + 3 * chan) % SAMPLES)
    freqs = jax.random.randint(keys[4], (12,), 1, SEG_LEN // 2)
    amps = jnp.exp(jax.random.uniform(keys[5], (12,), jnp.float32, math.log(0.5), math.log(4.0)))
    phases = jax.random.uniform(keys[6], (C, 12), jnp.float32, -math.pi, math.pi)

    def add_tone(index, total):
        step = jnp.take(freqs, index)
        angle = (times * step % SEG_LEN).astype(jnp.float32) * (2.0 * math.pi / SEG_LEN)
        shift = jnp.take(phases, index, axis=1)[:, None]
        return total + jnp.take(amps, index) * jnp.cos(angle + shift)
    tone = lax.fori_loop(0, 12, add_tone, jnp.zeros((C, SAMPLES), jnp.float32))
    signal = gain * (envelope * noise + wave + tone)
    return signal.reshape(C // CB, CB, SAMPLES).astype(jnp.bfloat16)


def with_ends(array, rng, least, high):
    place = [jax.random.randint(jax.random.fold_in(rng, axis), (), 0, length) for axis, length in enumerate(array.shape)]
    widest = array.shape.index(max(array.shape))
    neighbour = place[:widest] + [(place[widest] + 1) % array.shape[widest]] + place[widest + 1:]
    return array.at[tuple(place)].set(least).at[tuple(neighbour)].set(high)


def setup_inputs(seed: int = 0, part: int = 0) -> dict:
    splits = jax.random.split(jax.random.key(seed), 4)
    part_keys = jax.random.split(jax.random.fold_in(splits[3], part), 4)
    raw = draw_raw(jax.random.fold_in(jax.random.fold_in(splits[3], part), 71), part)
    valid = with_ends((jax.random.randint(part_keys[1], (N_BLK, CB), 0, 8) < 7).astype(jnp.int32), jax.random.fold_in(part_keys[1], 1), 0, 1)
    select = with_ends((jax.random.randint(part_keys[2], (N_BLK, N_BLK, SEG), 0, 4) < 3).astype(jnp.int32), jax.random.fold_in(part_keys[2], 1), 0, 1)
    return {"raw": raw, "valid": valid, "select": select}


eps = 1e-06

def dft_tables(length, bins):
    times = jnp.arange(length, dtype=jnp.int32)[:, None]
    freqs = jnp.arange(bins, dtype=jnp.int32)[None, :]
    angle = (times * freqs % length).astype(jnp.float32) * (2.0 * math.pi / length)
    return (jnp.cos(angle), -jnp.sin(angle))

def whiten(records, valid, seg_len, band):
    chans = records.shape[0] * records.shape[1]
    frames = records.astype(jnp.float32).reshape(chans, -1, seg_len)
    segs = frames.shape[1]
    bins = seg_len // 2
    cos_tab, sin_tab = dft_tables(seg_len, bins)
    real = jnp.einsum('cst,tf->csf', frames, cos_tab, precision=lax.Precision.HIGHEST)
    imag = jnp.einsum('cst,tf->csf', frames, sin_tab, precision=lax.Precision.HIGHEST)
    bands = bins // band
    power = (real * real + imag * imag).reshape(chans, segs, bands, band)
    level = lax.optimization_barrier(jnp.mean(power, axis=(1, 3)))
    factor = valid.reshape(chans, 1).astype(jnp.float32) / jnp.sqrt(level + eps)
    factor = factor[:, None, :, None]
    real = (real.reshape(chans, segs, bands, band) * factor).reshape(chans, segs, bins)
    imag = (imag.reshape(chans, segs, bands, band) * factor).reshape(chans, segs, bins)
    return jnp.stack([real, imag], axis=2).astype(jnp.bfloat16)

def lag_table(bins, lags, seg_len, scale):
    freqs = jnp.arange(bins, dtype=jnp.int32)[:, None]
    shifts = jnp.arange(lags, dtype=jnp.int32)[None, :] - lags // 2
    angle = (freqs * shifts % seg_len).astype(jnp.float32) * (2.0 * math.pi / seg_len)
    weight = jnp.where(freqs == 0, 1.0, 2.0).astype(jnp.float32) * scale
    return jnp.stack([weight * jnp.cos(angle), -weight * jnp.sin(angle)])

def cross(own, partner, weights):
    own_f = own.astype(jnp.float32)
    masked = partner.astype(jnp.float32) * weights.astype(jnp.float32)[:, None, :, None, None]

    def product(left, right):
        return jnp.einsum('isf,njsf->injf', left, right)
    real = product(own_f[:, :, 0], masked[:, :, :, 0]) + product(own_f[:, :, 1], masked[:, :, :, 1])
    imag = product(own_f[:, :, 1], masked[:, :, :, 0]) - product(own_f[:, :, 0], masked[:, :, :, 1])
    return (real, imag)

def reference(raw, valid, select):
    nblk, cblock, samples = raw.shape
    chans = nblk * cblock
    spectra = whiten(raw, valid, SEG_LEN, BAND)
    segs = spectra.shape[1]
    bins = SEG_LEN // 2
    table = lag_table(bins, LAGS, SEG_LEN, 1.0 / math.sqrt(bins * segs))
    blocks = spectra.reshape(nblk, cblock, segs, 2, bins)

    def one_block(item):
        own, weights = item
        real, imag = cross(own, blocks, weights)
        stacked = jnp.stack([real, imag], axis=3)
        return jnp.einsum('injrf,rfl->injl', stacked, table, precision=lax.Precision.HIGHEST)
    result = lax.map(one_block, (blocks, select))
    return result.reshape(chans, nblk, cblock, LAGS)
```

```python
import functools
import math

import jax
import jax.numpy as jnp
import numpy as np
from jax import lax
from jax.experimental import pallas as pl
from jax.experimental.pallas import tpu as pltpu
from jax.sharding import PartitionSpec as P

SEG_LEN = 1024
BAND = 64
LAGS = 512
BINS = SEG_LEN // 2

eps = 1e-06
MESH = pl.DeviceIdType.MESH


def split_table(table):
    high = table.astype(np.float32).astype(jnp.bfloat16)
    low = (table - high.astype(np.float64)).astype(np.float32).astype(jnp.bfloat16)
    return np.stack([high, low])


def dft_split():
    times = np.arange(SEG_LEN)[:, None]
    freqs = np.arange(BINS)[None, :]
    angle = (times * freqs % SEG_LEN) * (2.0 * math.pi / SEG_LEN)
    return split_table(np.concatenate([np.cos(angle), -np.sin(angle)], axis=1))


def lag_split(scale):
    freqs = np.arange(BINS)[:, None]
    shifts = np.arange(LAGS)[None, :] - LAGS // 2
    angle = (freqs * shifts % SEG_LEN) * (2.0 * math.pi / SEG_LEN)
    weight = np.where(freqs == 0, 1.0, 2.0) * scale
    return split_table(
        np.concatenate([weight * np.cos(angle), -weight * np.sin(angle)], axis=0)
    )


def band_ones():
    band = np.arange(256) // BAND
    return (band[:, None] == band[None, :]).astype(jnp.bfloat16)


def split(x):
    high = x.astype(jnp.bfloat16)
    low = (x - high.astype(jnp.float32)).astype(jnp.bfloat16)
    return high, low


def mxu(a, b):
    return jnp.dot(a, b, preferred_element_type=jnp.float32)


def kernel(
    nblk, nsub, wide,
    raw, valid, select, dft, lag, band, out,
    part, own, vpart, vown, x32, vcol, dft_v, lag_v, band_v,
    send, recv, vsend, vrecv, local, tabs,
):
    me_b, me_u = lax.axis_index("blk"), lax.axis_index("sub")
    rows = wide * nsub
    prow = wide * nblk
    tab_copies = [
        pltpu.make_async_copy(dft.at[0], dft_v.at[0], tabs.at[0]),
        pltpu.make_async_copy(dft.at[1], dft_v.at[1], tabs.at[1]),
        pltpu.make_async_copy(band, band_v, tabs.at[2]),
        pltpu.make_async_copy(lag, lag_v, tabs.at[3]),
    ]
    mine = [
        pltpu.make_async_copy(raw, part.at[me_b], local.at[0]),
        pltpu.make_async_copy(valid, vpart.at[me_b], local.at[1]),
        pltpu.make_async_copy(valid, vown.at[me_u], local.at[2]),
    ]
    offsets = [(db, du) for db in range(nblk) for du in range(nsub) if db or du]

    def device(db, du):
        return {"blk": lax.rem(me_b + db, nblk), "sub": lax.rem(me_u + du, nsub)}

    barrier = pltpu.get_barrier_semaphore()
    for db, du in offsets:
        pl.semaphore_signal(
            barrier, inc=1, device_id=device(db, du), device_id_type=MESH
        )
    for copy in mine + tab_copies:
        copy.start()
    pl.semaphore_wait(barrier, len(offsets))

    def exchange(db, du, at_b, at_u):
        there = device(db, du)
        index = db * nsub + du
        sems = dict(device_id=there, device_id_type=MESH)
        copies = []
        if du == 0:
            copies.append(pltpu.make_async_remote_copy(
                raw, part.at[at_b], send.at[index], recv.at[index], **sems))
            copies.append(pltpu.make_async_remote_copy(
                valid, vpart.at[at_b], vsend.at[index], vrecv.at[index], **sems))
        else:
            copies.append(pltpu.make_async_remote_copy(
                raw.at[there["blk"]], own.at[at_b, at_u],
                send.at[index], recv.at[index], **sems))
            if db == 0:
                copies.append(pltpu.make_async_remote_copy(
                    valid, vown.at[at_u], vsend.at[index], vrecv.at[index], **sems))
        return copies

    order = sorted(offsets, key=lambda o: (o[1] != 0, o))
    sent, landed = [], []
    for db, du in order:
        copies = exchange(db, du, me_b, me_u)
        for copy in copies:
            copy.start()
        sent += copies
        landed += exchange(
            db, du, lax.rem(me_b + nblk - db, nblk), lax.rem(me_u + nsub - du, nsub)
        )
    for copy in mine:
        copy.wait()
    for copy in landed:
        copy.wait_recv()

    for s in range(nblk):
        for n in range(nblk):
            x32[pl.ds(s * prow + n * wide, wide), :] = part[s, n].astype(jnp.float32)
    base = nblk * prow
    for s in range(nblk):
        for u in range(nsub):
            mine_here = part[s, me_b]
            piece = jnp.where(me_u == u, mine_here.astype(jnp.float32),
                              own[s, u].astype(jnp.float32))
            x32[pl.ds(base + s * rows + u * wide, wide), :] = piece
    for n in range(nblk):
        for k in range(wide):
            vcol[pl.ds(n * wide + k, 1), :] = jnp.broadcast_to(
                vpart[n][:, k : k + 1].astype(jnp.float32), (1, 128))
    for u in range(nsub):
        for k in range(wide):
            vcol[pl.ds(prow + u * wide + k, 1), :] = jnp.broadcast_to(
                vown[u][:, k : k + 1].astype(jnp.float32), (1, 128))
    for copy in tab_copies:
        copy.wait()

    x = x32[...].astype(jnp.bfloat16)
    spec = mxu(x, dft_v[0]) + mxu(x, dft_v[1])
    power = spec[:, :BINS] * spec[:, :BINS] + spec[:, BINS:] * spec[:, BINS:]
    ppow = sum(power[s * prow : (s + 1) * prow] for s in range(nblk))
    opow = sum(power[base + s * rows : base + (s + 1) * rows] for s in range(nblk))
    total = jnp.concatenate([ppow, opow], axis=0)
    high, low = split(total)
    both = jnp.concatenate([high, low], axis=0)
    sums = jnp.concatenate(
        [mxu(both[:, c : c + 256], band_v[...]) for c in range(0, BINS, 256)], axis=1)
    level = (sums[: prow + rows] + sums[prow + rows :]) * (1.0 / (BAND * nblk))
    factor = lax.rsqrt(level + eps) * jnp.tile(vcol[...], (1, BINS // 128))
    factor = jnp.concatenate([factor, factor], axis=1)
    fpart, fown = factor[:prow], factor[prow:]

    def rounded(v):
        return v.astype(jnp.bfloat16).astype(jnp.float32)

    acc_re = [0.0] * rows
    acc_im = [0.0] * rows
    row_id = lax.broadcasted_iota(jnp.int32, (prow, 1), 0) // wide
    for s in range(nblk):
        b = rounded(spec[s * prow : (s + 1) * prow] * fpart)
        a = rounded(spec[base + s * rows : base + (s + 1) * rows] * fown)
        w = jnp.zeros((prow, 1), jnp.float32)
        for n in range(nblk):
            w = jnp.where(row_id == n, select[0, n, s].astype(jnp.float32), w)
        b = b * w
        br, bi = b[:, :BINS], b[:, BINS:]
        for i in range(rows):
            ar, ai = a[i : i + 1, :BINS], a[i : i + 1, BINS:]
            acc_re[i] = acc_re[i] + (ar * br + ai * bi)
            acc_im[i] = acc_im[i] + (ai * br - ar * bi)
    stacked = jnp.concatenate(
        [jnp.concatenate(acc_re, axis=0), jnp.concatenate(acc_im, axis=0)], axis=1)
    high, low = split(stacked)
    count = rows * prow
    first = mxu(jnp.concatenate([high, low], axis=0), lag_v[0])
    out[...] = first[:count] + first[count:] + mxu(high, lag_v[1])
    for copy in sent:
        copy.wait_send()


def fused(nblk, nsub, raw, valid, select):
    wide = raw.shape[1]
    rows, prow = wide * nsub, wide * nblk
    tables = (
        jnp.asarray(dft_split()),
        jnp.asarray(lag_split(1.0 / math.sqrt(BINS * nblk))),
        jnp.asarray(band_ones()),
    )
    hbm = pl.BlockSpec(memory_space=pl.ANY)
    total = nblk * nsub
    result = pl.pallas_call(
        functools.partial(kernel, nblk, nsub, wide),
        out_shape=jax.ShapeDtypeStruct((rows * prow, LAGS), jnp.float32),
        in_specs=[hbm, hbm, pl.BlockSpec(memory_space=pltpu.SMEM), hbm, hbm, hbm],
        out_specs=pl.BlockSpec(memory_space=pltpu.VMEM),
        scratch_shapes=[
            pltpu.VMEM((nblk, nblk, wide, SEG_LEN), jnp.bfloat16),
            pltpu.VMEM((nblk, nsub, wide, SEG_LEN), jnp.bfloat16),
            pltpu.VMEM((nblk, 1, wide), jnp.int32),
            pltpu.VMEM((nsub, 1, wide), jnp.int32),
            pltpu.VMEM((nblk * (rows + prow), SEG_LEN), jnp.float32),
            pltpu.VMEM((rows + prow, 128), jnp.float32),
            pltpu.VMEM((2, SEG_LEN, 2 * BINS), jnp.bfloat16),
            pltpu.VMEM((2, 2 * BINS, LAGS), jnp.bfloat16),
            pltpu.VMEM((256, 256), jnp.bfloat16),
            pltpu.SemaphoreType.DMA((total,)),
            pltpu.SemaphoreType.DMA((total,)),
            pltpu.SemaphoreType.DMA((total,)),
            pltpu.SemaphoreType.DMA((total,)),
            pltpu.SemaphoreType.DMA((3,)),
            pltpu.SemaphoreType.DMA((4,)),
        ],
        compiler_params=pltpu.CompilerParams(
            collective_id=0, has_side_effects=True, vmem_limit_bytes=32 * 2**20
        ),
    )(raw, valid, select, *tables)
    return result.reshape(rows, nblk, wide, LAGS)


def dft_tables(length, bins):
    times = jnp.arange(length, dtype=jnp.int32)[:, None]
    freqs = jnp.arange(bins, dtype=jnp.int32)[None, :]
    angle = (times * freqs % length).astype(jnp.float32) * (2.0 * math.pi / length)
    return (jnp.cos(angle), -jnp.sin(angle))


def whiten(records, valid, seg_len, band):
    chans = records.shape[0] * records.shape[1]
    frames = records.astype(jnp.float32).reshape(chans, -1, seg_len)
    segs = frames.shape[1]
    bins = seg_len // 2
    cos_tab, sin_tab = dft_tables(seg_len, bins)
    real = jnp.einsum("cst,tf->csf", frames, cos_tab, precision=lax.Precision.HIGHEST)
    imag = jnp.einsum("cst,tf->csf", frames, sin_tab, precision=lax.Precision.HIGHEST)
    bands = bins // band
    power = (real * real + imag * imag).reshape(chans, segs, bands, band)
    level = jnp.mean(power, axis=(1, 3))
    factor = valid.reshape(chans, 1).astype(jnp.float32) / jnp.sqrt(level + eps)
    factor = factor[:, None, :, None]
    real = (real.reshape(chans, segs, bands, band) * factor).reshape(chans, segs, bins)
    imag = (imag.reshape(chans, segs, bands, band) * factor).reshape(chans, segs, bins)
    return jnp.stack([real, imag], axis=2).astype(jnp.bfloat16)


def lag_table(bins, lags, seg_len, scale):
    freqs = jnp.arange(bins, dtype=jnp.int32)[:, None]
    shifts = jnp.arange(lags, dtype=jnp.int32)[None, :] - lags // 2
    angle = (freqs * shifts % seg_len).astype(jnp.float32) * (2.0 * math.pi / seg_len)
    weight = jnp.where(freqs == 0, 1.0, 2.0).astype(jnp.float32) * scale
    return jnp.stack([weight * jnp.cos(angle), -weight * jnp.sin(angle)])


def pair_terms(own, weight_rows, piece):
    masked = piece * weight_rows.astype(jnp.bfloat16)[:, None, :, None, None]
    prod = jnp.einsum("isaf,njsbf->injabf", own, masked, preferred_element_type=jnp.float32)
    real = prod[:, :, :, 0, 0] + prod[:, :, :, 1, 1]
    imag = prod[:, :, :, 1, 0] - prod[:, :, :, 0, 1]
    return jnp.stack([real, imag], axis=3)


def by_collectives(raw, valid, select):
    regrouped = lax.all_to_all(raw, "blk", split_axis=0, concat_axis=2, tiled=True)
    spectra = whiten(regrouped, valid, SEG_LEN, BAND)
    segs = spectra.shape[1]
    table = lag_table(BINS, LAGS, SEG_LEN, 1.0 / math.sqrt(BINS * segs))
    block = lax.all_gather(spectra, "sub", axis=0, tiled=True)
    stacked = pair_terms(
        block, select[0], lax.all_gather(spectra[None], "blk", axis=0, tiled=True)
    )
    return jnp.einsum("injrf,rfl->injl", stacked, table, precision=lax.Precision.HIGHEST)


def solution(mesh):
    nblk, nsub = mesh.shape["blk"], mesh.shape["sub"]

    def per_device(raw, valid, select):
        fits = raw.shape[2] == SEG_LEN and raw.shape[0] == nblk and nblk * nsub <= 16
        if fits:
            return fused(nblk, nsub, raw, valid, select)
        return by_collectives(raw, valid, select)

    return jax.shard_map(
        per_device,
        mesh=mesh,
        in_specs=(
            P("cable", "sub", "blk"),
            P(("cable", "blk"), "sub"),
            P(("cable", "blk"), None, None),
        ),
        out_specs=P(("cable", "blk"), None, "sub", None),
        check_vma=False,
    )
```

```python
import functools
import math

import jax
import jax.numpy as jnp
import numpy as np
from jax import lax
from jax.experimental import pallas as pl
from jax.experimental.pallas import tpu as pltpu
from jax.sharding import PartitionSpec as P

SEG_LEN = 1024
BAND = 64
LAGS = 512
BINS = SEG_LEN // 2

eps = 1e-06
MESH = pl.DeviceIdType.MESH


def split_table(table):
    high = table.astype(np.float32).astype(jnp.bfloat16)
    low = (table - high.astype(np.float64)).astype(np.float32).astype(jnp.bfloat16)
    return np.stack([high, low])


def dft_split():
    times = np.arange(SEG_LEN)[:, None]
    freqs = np.arange(BINS)[None, :]
    angle = (times * freqs % SEG_LEN) * (2.0 * math.pi / SEG_LEN)
    return split_table(np.concatenate([np.cos(angle), -np.sin(angle)], axis=1))


def lag_split(scale):
    freqs = np.arange(BINS)[:, None]
    shifts = np.arange(LAGS)[None, :] - LAGS // 2
    angle = (freqs * shifts % SEG_LEN) * (2.0 * math.pi / SEG_LEN)
    weight = np.where(freqs == 0, 1.0, 2.0) * scale
    return split_table(
        np.concatenate([weight * np.cos(angle), -weight * np.sin(angle)], axis=0)
    )


def band_ones():
    band = np.arange(256) // BAND
    return (band[:, None] == band[None, :]).astype(jnp.bfloat16)


def split(x):
    high = x.astype(jnp.bfloat16)
    low = (x - high.astype(jnp.float32)).astype(jnp.bfloat16)
    return high, low


def mxu(a, b):
    return jnp.dot(a, b, preferred_element_type=jnp.float32)


def kernel(
    nblk, nsub, wide,
    raw, valid, choose, dft, lag, band, out,
    select, part, own, vpart, vown, x32, vcol, dft_v, lag_v, band_v,
    send, recv, vsend, vrecv, local, tabs,
):
    me_b, me_u = lax.axis_index("blk"), lax.axis_index("sub")
    rows = wide * nsub
    prow = wide * nblk
    tab_copies = [
        pltpu.make_async_copy(dft.at[0], dft_v.at[0], tabs.at[0]),
        pltpu.make_async_copy(dft.at[1], dft_v.at[1], tabs.at[1]),
        pltpu.make_async_copy(band, band_v, tabs.at[2]),
        pltpu.make_async_copy(lag, lag_v, tabs.at[3]),
    ]
    mine = [
        pltpu.make_async_copy(raw, part.at[me_b], local.at[0]),
        pltpu.make_async_copy(valid, vpart.at[me_b], local.at[1]),
        pltpu.make_async_copy(valid, vown.at[me_u], local.at[2]),
        pltpu.make_async_copy(choose, select, local.at[3]),
    ]
    offsets = [(db, du) for db in range(nblk) for du in range(nsub) if db or du]

    def device(db, du):
        return {"blk": lax.rem(me_b + db, nblk), "sub": lax.rem(me_u + du, nsub)}

    barrier = pltpu.get_barrier_semaphore()
    for db, du in offsets:
        pl.semaphore_signal(
            barrier, inc=1, device_id=device(db, du), device_id_type=MESH
        )
    for copy in mine + tab_copies:
        copy.start()
    pl.semaphore_wait(barrier, len(offsets))

    def exchange(db, du, at_b, at_u):
        there = device(db, du)
        index = db * nsub + du
        sems = dict(device_id=there, device_id_type=MESH)
        copies = []
        if du == 0:
            copies.append(pltpu.make_async_remote_copy(
                raw, part.at[at_b], send.at[index], recv.at[index], **sems))
            copies.append(pltpu.make_async_remote_copy(
                valid, vpart.at[at_b], vsend.at[index], vrecv.at[index], **sems))
        else:
            copies.append(pltpu.make_async_remote_copy(
                raw.at[there["blk"]], own.at[at_b, at_u],
                send.at[index], recv.at[index], **sems))
            if db == 0:
                copies.append(pltpu.make_async_remote_copy(
                    valid, vown.at[at_u], vsend.at[index], vrecv.at[index], **sems))
        return copies

    order = sorted(offsets, key=lambda o: (o[1] != 0, o))
    sent, landed = [], []
    for db, du in order:
        copies = exchange(db, du, me_b, me_u)
        for copy in copies:
            copy.start()
        sent += copies
        landed += exchange(
            db, du, lax.rem(me_b + nblk - db, nblk), lax.rem(me_u + nsub - du, nsub)
        )
    for copy in mine:
        copy.wait()
    for copy in landed:
        copy.wait_recv()

    for s in range(nblk):
        for n in range(nblk):
            x32[pl.ds(s * prow + n * wide, wide), :] = part[s, n].astype(jnp.float32)
    base = nblk * prow
    for s in range(nblk):
        for u in range(nsub):
            mine_here = part[s, me_b]
            piece = jnp.where(me_u == u, mine_here.astype(jnp.float32),
                              own[s, u].astype(jnp.float32))
            x32[pl.ds(base + s * rows + u * wide, wide), :] = piece
    for n in range(nblk):
        for k in range(wide):
            vcol[pl.ds(n * wide + k, 1), :] = jnp.broadcast_to(
                vpart[n][:, k : k + 1].astype(jnp.float32), (1, 128))
    for u in range(nsub):
        for k in range(wide):
            vcol[pl.ds(prow + u * wide + k, 1), :] = jnp.broadcast_to(
                vown[u][:, k : k + 1].astype(jnp.float32), (1, 128))
    for copy in tab_copies:
        copy.wait()

    x = x32[...].astype(jnp.bfloat16)
    spec = mxu(x, dft_v[0]) + mxu(x, dft_v[1])
    power = spec[:, :BINS] * spec[:, :BINS] + spec[:, BINS:] * spec[:, BINS:]
    ppow = sum(power[s * prow : (s + 1) * prow] for s in range(nblk))
    opow = sum(power[base + s * rows : base + (s + 1) * rows] for s in range(nblk))
    total = jnp.concatenate([ppow, opow], axis=0)
    high, low = split(total)
    both = jnp.concatenate([high, low], axis=0)
    sums = jnp.concatenate(
        [mxu(both[:, c : c + 256], band_v[...]) for c in range(0, BINS, 256)], axis=1)
    level = (sums[: prow + rows] + sums[prow + rows :]) * (1.0 / (BAND * nblk))
    factor = lax.rsqrt(level + eps) * jnp.tile(vcol[...], (1, BINS // 128))
    factor = jnp.concatenate([factor, factor], axis=1)
    fpart, fown = factor[:prow], factor[prow:]

    def rounded(v):
        return v.astype(jnp.bfloat16).astype(jnp.float32)

    acc_re = [0.0] * rows
    acc_im = [0.0] * rows
    row_id = lax.broadcasted_iota(jnp.int32, (prow, 1), 0) // wide
    for s in range(nblk):
        b = rounded(spec[s * prow : (s + 1) * prow] * fpart)
        a = rounded(spec[base + s * rows : base + (s + 1) * rows] * fown)
        w = jnp.zeros((prow, 1), jnp.float32)
        for n in range(nblk):
            w = jnp.where(row_id == n, select[0, n, s].astype(jnp.float32), w)
        b = b * w
        br, bi = b[:, :BINS], b[:, BINS:]
        for i in range(rows):
            ar, ai = a[i : i + 1, :BINS], a[i : i + 1, BINS:]
            acc_re[i] = acc_re[i] + (ar * br + ai * bi)
            acc_im[i] = acc_im[i] + (ai * br - ar * bi)
    stacked = jnp.concatenate(
        [jnp.concatenate(acc_re, axis=0), jnp.concatenate(acc_im, axis=0)], axis=1)
    high, low = split(stacked)
    count = rows * prow
    first = mxu(jnp.concatenate([high, low], axis=0), lag_v[0])
    out[...] = first[:count] + first[count:] + mxu(high, lag_v[1])
    for copy in sent:
        copy.wait_send()


def fused(nblk, nsub, raw, valid, select):
    wide = raw.shape[1]
    rows, prow = wide * nsub, wide * nblk
    tables = (
        jnp.asarray(dft_split()),
        jnp.asarray(lag_split(1.0 / math.sqrt(BINS * nblk))),
        jnp.asarray(band_ones()),
    )
    hbm = pl.BlockSpec(memory_space=pltpu.HBM)
    total = nblk * nsub
    result = pl.pallas_call(
        functools.partial(kernel, nblk, nsub, wide),
        out_shape=jax.ShapeDtypeStruct((rows * prow, LAGS), jnp.float32),
        in_specs=[hbm] * 6,
        out_specs=pl.BlockSpec(memory_space=pltpu.VMEM),
        scratch_shapes=[
            pltpu.SMEM(select.shape, jnp.int32),
            pltpu.VMEM((nblk, nblk, wide, SEG_LEN), jnp.bfloat16),
            pltpu.VMEM((nblk, nsub, wide, SEG_LEN), jnp.bfloat16),
            pltpu.VMEM((nblk, 1, wide), jnp.int32),
            pltpu.VMEM((nsub, 1, wide), jnp.int32),
            pltpu.VMEM((nblk * (rows + prow), SEG_LEN), jnp.float32),
            pltpu.VMEM((rows + prow, 128), jnp.float32),
            pltpu.VMEM((2, SEG_LEN, 2 * BINS), jnp.bfloat16),
            pltpu.VMEM((2, 2 * BINS, LAGS), jnp.bfloat16),
            pltpu.VMEM((256, 256), jnp.bfloat16),
            pltpu.SemaphoreType.DMA((total,)),
            pltpu.SemaphoreType.DMA((total,)),
            pltpu.SemaphoreType.DMA((total,)),
            pltpu.SemaphoreType.DMA((total,)),
            pltpu.SemaphoreType.DMA((4,)),
            pltpu.SemaphoreType.DMA((4,)),
        ],
        compiler_params=pltpu.CompilerParams(
            collective_id=0, has_side_effects=True, vmem_limit_bytes=32 * 2**20
        ),
    )(raw, valid, select, *tables)
    return result.reshape(rows, nblk, wide, LAGS)


def dft_tables(length, bins):
    times = jnp.arange(length, dtype=jnp.int32)[:, None]
    freqs = jnp.arange(bins, dtype=jnp.int32)[None, :]
    angle = (times * freqs % length).astype(jnp.float32) * (2.0 * math.pi / length)
    return (jnp.cos(angle), -jnp.sin(angle))


def whiten(records, valid, seg_len, band):
    chans = records.shape[0] * records.shape[1]
    frames = records.astype(jnp.float32).reshape(chans, -1, seg_len)
    segs = frames.shape[1]
    bins = seg_len // 2
    cos_tab, sin_tab = dft_tables(seg_len, bins)
    real = jnp.einsum("cst,tf->csf", frames, cos_tab, precision=lax.Precision.HIGHEST)
    imag = jnp.einsum("cst,tf->csf", frames, sin_tab, precision=lax.Precision.HIGHEST)
    bands = bins // band
    power = (real * real + imag * imag).reshape(chans, segs, bands, band)
    level = jnp.mean(power, axis=(1, 3))
    factor = valid.reshape(chans, 1).astype(jnp.float32) / jnp.sqrt(level + eps)
    factor = factor[:, None, :, None]
    real = (real.reshape(chans, segs, bands, band) * factor).reshape(chans, segs, bins)
    imag = (imag.reshape(chans, segs, bands, band) * factor).reshape(chans, segs, bins)
    return jnp.stack([real, imag], axis=2).astype(jnp.bfloat16)


def lag_table(bins, lags, seg_len, scale):
    freqs = jnp.arange(bins, dtype=jnp.int32)[:, None]
    shifts = jnp.arange(lags, dtype=jnp.int32)[None, :] - lags // 2
    angle = (freqs * shifts % seg_len).astype(jnp.float32) * (2.0 * math.pi / seg_len)
    weight = jnp.where(freqs == 0, 1.0, 2.0).astype(jnp.float32) * scale
    return jnp.stack([weight * jnp.cos(angle), -weight * jnp.sin(angle)])


def pair_terms(own, weight_rows, piece):
    masked = piece * weight_rows.astype(jnp.bfloat16)[:, None, :, None, None]
    prod = jnp.einsum("isaf,njsbf->injabf", own, masked, preferred_element_type=jnp.float32)
    real = prod[:, :, :, 0, 0] + prod[:, :, :, 1, 1]
    imag = prod[:, :, :, 1, 0] - prod[:, :, :, 0, 1]
    return jnp.stack([real, imag], axis=3)


def by_collectives(raw, valid, select):
    regrouped = lax.all_to_all(raw, "blk", split_axis=0, concat_axis=2, tiled=True)
    spectra = whiten(regrouped, valid, SEG_LEN, BAND)
    segs = spectra.shape[1]
    table = lag_table(BINS, LAGS, SEG_LEN, 1.0 / math.sqrt(BINS * segs))
    block = lax.all_gather(spectra, "sub", axis=0, tiled=True)
    stacked = pair_terms(
        block, select[0], lax.all_gather(spectra[None], "blk", axis=0, tiled=True)
    )
    return jnp.einsum("injrf,rfl->injl", stacked, table, precision=lax.Precision.HIGHEST)


def solution(mesh):
    nblk, nsub = mesh.shape["blk"], mesh.shape["sub"]

    def per_device(raw, valid, select):
        fits = raw.shape[2] == SEG_LEN and raw.shape[0] == nblk and nblk * nsub <= 16
        if fits:
            return fused(nblk, nsub, raw, valid, select)
        return by_collectives(raw, valid, select)

    return jax.shard_map(
        per_device,
        mesh=mesh,
        in_specs=(
            P("cable", "sub", "blk"),
            P(("cable", "blk"), "sub"),
            P(("cable", "blk"), None, None),
        ),
        out_specs=P(("cable", "blk"), None, "sub", None),
        check_vma=False,
    )
```

```python
import functools
import math

import jax
import jax.numpy as jnp
import numpy as np
from jax import lax
from jax.experimental import pallas as pl
from jax.experimental.pallas import tpu as pltpu
from jax.sharding import PartitionSpec as P

SEG_LEN = 1024
BAND = 64
LAGS = 512
BINS = SEG_LEN // 2

eps = 1e-06
MESH = pl.DeviceIdType.MESH


def split_table(table):
    high = table.astype(np.float32).astype(jnp.bfloat16)
    low = (table - high.astype(np.float64)).astype(np.float32).astype(jnp.bfloat16)
    return np.stack([high, low])


def dft_split():
    times = np.arange(SEG_LEN)[:, None]
    freqs = np.arange(BINS)[None, :]
    angle = (times * freqs % SEG_LEN) * (2.0 * math.pi / SEG_LEN)
    return split_table(np.concatenate([np.cos(angle), -np.sin(angle)], axis=1))


def lag_split(scale):
    freqs = np.arange(BINS)[:, None]
    shifts = np.arange(LAGS)[None, :] - LAGS // 2
    angle = (freqs * shifts % SEG_LEN) * (2.0 * math.pi / SEG_LEN)
    weight = np.where(freqs == 0, 1.0, 2.0) * scale
    return split_table(
        np.concatenate([weight * np.cos(angle), -weight * np.sin(angle)], axis=0)
    )


def band_ones():
    first = lax.broadcasted_iota(jnp.int32, (256, 256), 0) // BAND
    second = lax.broadcasted_iota(jnp.int32, (256, 256), 1) // BAND
    return jnp.where(first == second, 1.0, 0.0).astype(jnp.bfloat16)


def split(x):
    high = x.astype(jnp.bfloat16)
    low = (x - high.astype(jnp.float32)).astype(jnp.bfloat16)
    return high, low


def mxu(a, b):
    return jnp.dot(a, b, preferred_element_type=jnp.float32)


def kernel(
    nblk, nsub, wide,
    raw, valid, choose, dft, lag, out,
    select, part, own, vpart, vown, x32, vcol, dft_v, lag_v,
    send, recv, vsend, vrecv, local, tabs,
):
    me_b, me_u = lax.axis_index("blk"), lax.axis_index("sub")
    rows = wide * nsub
    prow = wide * nblk
    tab_copies = [
        pltpu.make_async_copy(dft.at[0], dft_v.at[0], tabs.at[0]),
        pltpu.make_async_copy(dft.at[1], dft_v.at[1], tabs.at[1]),
        pltpu.make_async_copy(lag, lag_v, tabs.at[2]),
    ]
    mine = [
        pltpu.make_async_copy(raw, part.at[me_b], local.at[0]),
        pltpu.make_async_copy(valid, vpart.at[me_b], local.at[1]),
        pltpu.make_async_copy(valid, vown.at[me_u], local.at[2]),
        pltpu.make_async_copy(choose, select, local.at[3]),
    ]
    offsets = [(db, du) for db in range(nblk) for du in range(nsub) if db or du]

    def device(db, du):
        return {"blk": lax.rem(me_b + db, nblk), "sub": lax.rem(me_u + du, nsub)}

    barrier = pltpu.get_barrier_semaphore()
    for db, du in offsets:
        pl.semaphore_signal(
            barrier, inc=1, device_id=device(db, du), device_id_type=MESH
        )
    pl.semaphore_wait(barrier, len(offsets))

    def exchange(db, du, at_b, at_u):
        there = device(db, du)
        index = db * nsub + du
        sems = dict(device_id=there, device_id_type=MESH)
        copies = []
        if du == 0:
            copies.append(pltpu.make_async_remote_copy(
                raw, part.at[at_b], send.at[index], recv.at[index], **sems))
            copies.append(pltpu.make_async_remote_copy(
                valid, vpart.at[at_b], vsend.at[index], vrecv.at[index], **sems))
        else:
            copies.append(pltpu.make_async_remote_copy(
                raw.at[there["blk"]], own.at[at_b, at_u],
                send.at[index], recv.at[index], **sems))
            if db == 0:
                copies.append(pltpu.make_async_remote_copy(
                    valid, vown.at[at_u], vsend.at[index], vrecv.at[index], **sems))
        return copies

    order = sorted(offsets, key=lambda o: (o[1] != 0, o))
    sent, landed = [], []
    for db, du in order:
        copies = exchange(db, du, me_b, me_u)
        for copy in copies:
            copy.start()
        sent += copies
        landed += exchange(
            db, du, lax.rem(me_b + nblk - db, nblk), lax.rem(me_u + nsub - du, nsub)
        )
    for copy in mine + tab_copies:
        copy.start()
    for copy in mine:
        copy.wait()
    for copy in landed:
        copy.wait_recv()

    for s in range(nblk):
        for n in range(nblk):
            x32[pl.ds(s * prow + n * wide, wide), :] = part[s, n].astype(jnp.float32)
    base = nblk * prow
    for s in range(nblk):
        for u in range(nsub):
            mine_here = part[s, me_b]
            piece = jnp.where(me_u == u, mine_here.astype(jnp.float32),
                              own[s, u].astype(jnp.float32))
            x32[pl.ds(base + s * rows + u * wide, wide), :] = piece
    for n in range(nblk):
        for k in range(wide):
            vcol[pl.ds(n * wide + k, 1), :] = jnp.broadcast_to(
                vpart[n][:, k : k + 1].astype(jnp.float32), (1, 128))
    for u in range(nsub):
        for k in range(wide):
            vcol[pl.ds(prow + u * wide + k, 1), :] = jnp.broadcast_to(
                vown[u][:, k : k + 1].astype(jnp.float32), (1, 128))
    for copy in tab_copies:
        copy.wait()

    x = x32[...].astype(jnp.bfloat16)
    spec = mxu(x, dft_v[0]) + mxu(x, dft_v[1])
    power = spec[:, :BINS] * spec[:, :BINS] + spec[:, BINS:] * spec[:, BINS:]
    ppow = sum(power[s * prow : (s + 1) * prow] for s in range(nblk))
    opow = sum(power[base + s * rows : base + (s + 1) * rows] for s in range(nblk))
    total = jnp.concatenate([ppow, opow], axis=0)
    ones = band_ones()
    high, low = split(total)
    both = jnp.concatenate([high, low], axis=0)
    sums = jnp.concatenate(
        [mxu(both[:, c : c + 256], ones) for c in range(0, BINS, 256)], axis=1)
    level = (sums[: prow + rows] + sums[prow + rows :]) * (1.0 / (BAND * nblk))
    factor = lax.rsqrt(level + eps) * jnp.tile(vcol[...], (1, BINS // 128))
    factor = jnp.concatenate([factor, factor], axis=1)
    fpart, fown = factor[:prow], factor[prow:]

    def rounded(v):
        return v.astype(jnp.bfloat16).astype(jnp.float32)

    acc_re = [0.0] * rows
    acc_im = [0.0] * rows
    row_id = lax.broadcasted_iota(jnp.int32, (prow, 1), 0) // wide
    for s in range(nblk):
        b = rounded(spec[s * prow : (s + 1) * prow] * fpart)
        a = rounded(spec[base + s * rows : base + (s + 1) * rows] * fown)
        w = jnp.zeros((prow, 1), jnp.float32)
        for n in range(nblk):
            w = jnp.where(row_id == n, select[0, n, s].astype(jnp.float32), w)
        b = b * w
        br, bi = b[:, :BINS], b[:, BINS:]
        for i in range(rows):
            ar, ai = a[i : i + 1, :BINS], a[i : i + 1, BINS:]
            acc_re[i] = acc_re[i] + (ar * br + ai * bi)
            acc_im[i] = acc_im[i] + (ai * br - ar * bi)
    stacked = jnp.concatenate(
        [jnp.concatenate(acc_re, axis=0), jnp.concatenate(acc_im, axis=0)], axis=1)
    high, low = split(stacked)
    count = rows * prow
    first = mxu(jnp.concatenate([high, low], axis=0), lag_v[0])
    out[...] = first[:count] + first[count:] + mxu(high, lag_v[1])
    for copy in sent:
        copy.wait_send()


def fused(nblk, nsub, raw, valid, select):
    wide = raw.shape[1]
    rows, prow = wide * nsub, wide * nblk
    tables = (
        jnp.asarray(dft_split()),
        jnp.asarray(lag_split(1.0 / math.sqrt(BINS * nblk))),
    )
    hbm = pl.BlockSpec(memory_space=pltpu.HBM)
    total = nblk * nsub
    result = pl.pallas_call(
        functools.partial(kernel, nblk, nsub, wide),
        out_shape=jax.ShapeDtypeStruct((rows * prow, LAGS), jnp.float32),
        in_specs=[hbm] * 5,
        out_specs=pl.BlockSpec(memory_space=pltpu.VMEM),
        scratch_shapes=[
            pltpu.SMEM(select.shape, jnp.int32),
            pltpu.VMEM((nblk, nblk, wide, SEG_LEN), jnp.bfloat16),
            pltpu.VMEM((nblk, nsub, wide, SEG_LEN), jnp.bfloat16),
            pltpu.VMEM((nblk, 1, wide), jnp.int32),
            pltpu.VMEM((nsub, 1, wide), jnp.int32),
            pltpu.VMEM((nblk * (rows + prow), SEG_LEN), jnp.float32),
            pltpu.VMEM((rows + prow, 128), jnp.float32),
            pltpu.VMEM((2, SEG_LEN, 2 * BINS), jnp.bfloat16),
            pltpu.VMEM((2, 2 * BINS, LAGS), jnp.bfloat16),
            pltpu.SemaphoreType.DMA((total,)),
            pltpu.SemaphoreType.DMA((total,)),
            pltpu.SemaphoreType.DMA((total,)),
            pltpu.SemaphoreType.DMA((total,)),
            pltpu.SemaphoreType.DMA((4,)),
            pltpu.SemaphoreType.DMA((3,)),
        ],
        compiler_params=pltpu.CompilerParams(
            collective_id=0, has_side_effects=True, vmem_limit_bytes=32 * 2**20
        ),
    )(*(pltpu.with_memory_space_constraint(a, pltpu.HBM) for a in (raw, valid, select) + tables))
    return result.reshape(rows, nblk, wide, LAGS)


def dft_tables(length, bins):
    times = jnp.arange(length, dtype=jnp.int32)[:, None]
    freqs = jnp.arange(bins, dtype=jnp.int32)[None, :]
    angle = (times * freqs % length).astype(jnp.float32) * (2.0 * math.pi / length)
    return (jnp.cos(angle), -jnp.sin(angle))


def whiten(records, valid, seg_len, band):
    chans = records.shape[0] * records.shape[1]
    frames = records.astype(jnp.float32).reshape(chans, -1, seg_len)
    segs = frames.shape[1]
    bins = seg_len // 2
    cos_tab, sin_tab = dft_tables(seg_len, bins)
    real = jnp.einsum("cst,tf->csf", frames, cos_tab, precision=lax.Precision.HIGHEST)
    imag = jnp.einsum("cst,tf->csf", frames, sin_tab, precision=lax.Precision.HIGHEST)
    bands = bins // band
    power = (real * real + imag * imag).reshape(chans, segs, bands, band)
    level = jnp.mean(power, axis=(1, 3))
    factor = valid.reshape(chans, 1).astype(jnp.float32) / jnp.sqrt(level + eps)
    factor = factor[:, None, :, None]
    real = (real.reshape(chans, segs, bands, band) * factor).reshape(chans, segs, bins)
    imag = (imag.reshape(chans, segs, bands, band) * factor).reshape(chans, segs, bins)
    return jnp.stack([real, imag], axis=2).astype(jnp.bfloat16)


def lag_table(bins, lags, seg_len, scale):
    freqs = jnp.arange(bins, dtype=jnp.int32)[:, None]
    shifts = jnp.arange(lags, dtype=jnp.int32)[None, :] - lags // 2
    angle = (freqs * shifts % seg_len).astype(jnp.float32) * (2.0 * math.pi / seg_len)
    weight = jnp.where(freqs == 0, 1.0, 2.0).astype(jnp.float32) * scale
    return jnp.stack([weight * jnp.cos(angle), -weight * jnp.sin(angle)])


def pair_terms(own, weight_rows, piece):
    masked = piece * weight_rows.astype(jnp.bfloat16)[:, None, :, None, None]
    prod = jnp.einsum("isaf,njsbf->injabf", own, masked, preferred_element_type=jnp.float32)
    real = prod[:, :, :, 0, 0] + prod[:, :, :, 1, 1]
    imag = prod[:, :, :, 1, 0] - prod[:, :, :, 0, 1]
    return jnp.stack([real, imag], axis=3)


def by_collectives(raw, valid, select):
    regrouped = lax.all_to_all(raw, "blk", split_axis=0, concat_axis=2, tiled=True)
    spectra = whiten(regrouped, valid, SEG_LEN, BAND)
    segs = spectra.shape[1]
    table = lag_table(BINS, LAGS, SEG_LEN, 1.0 / math.sqrt(BINS * segs))
    block = lax.all_gather(spectra, "sub", axis=0, tiled=True)
    stacked = pair_terms(
        block, select[0], lax.all_gather(spectra[None], "blk", axis=0, tiled=True)
    )
    return jnp.einsum("injrf,rfl->injl", stacked, table, precision=lax.Precision.HIGHEST)


def solution(mesh):
    nblk, nsub = mesh.shape["blk"], mesh.shape["sub"]

    def per_device(raw, valid, select):
        fits = raw.shape[2] == SEG_LEN and raw.shape[0] == nblk and nblk * nsub <= 16
        if fits:
            return fused(nblk, nsub, raw, valid, select)
        return by_collectives(raw, valid, select)

    return jax.shard_map(
        per_device,
        mesh=mesh,
        in_specs=(
            P("cable", "sub", "blk"),
            P(("cable", "blk"), "sub"),
            P(("cable", "blk"), None, None),
        ),
        out_specs=P(("cable", "blk"), None, "sub", None),
        check_vma=False,
    )
```

```python
import functools
import math

import jax
import jax.numpy as jnp
import numpy as np
from jax import lax
from jax.experimental import pallas as pl
from jax.experimental.pallas import tpu as pltpu
from jax.sharding import PartitionSpec as P

SEG_LEN = 1024
BAND = 64
LAGS = 512
BINS = SEG_LEN // 2
QUARTER = SEG_LEN // 4
GROUP = BINS // 4

eps = 1e-06
MESH = pl.DeviceIdType.MESH


def split_table(table):
    high = table.astype(np.float32).astype(jnp.bfloat16)
    low = (table - high.astype(np.float64)).astype(np.float32).astype(jnp.bfloat16)
    return np.stack([high, low])


def waves(freqs, times):
    angle = (freqs * times % SEG_LEN) * (2.0 * math.pi / SEG_LEN)
    return np.cos(angle), -np.sin(angle)


def bins_of(*classes):
    return np.concatenate([np.arange(r, BINS, 4) for r in classes])


def dft_split():
    def table(length, *classes):
        freqs = bins_of(*classes)[None, :]
        return np.concatenate(waves(freqs, np.arange(length)[:, None]), axis=1)

    even = np.concatenate([table(QUARTER, 0), table(QUARTER, 2)], axis=1)
    return split_table(np.concatenate([even, table(2 * QUARTER, 1, 3)], axis=0))


def lag_split(scale):
    def table(count, *classes):
        freqs = bins_of(*classes)[:, None]
        weight = np.where(freqs == 0, 1.0, 2.0) * scale
        shifts = np.arange(count)[None, :] - LAGS // 2
        return np.concatenate([weight * w for w in waves(freqs, shifts)], axis=0)

    even = np.concatenate([table(LAGS // 2, 0), table(LAGS // 2, 2)], axis=1)
    return split_table(np.concatenate([even, table(LAGS, 1, 3)], axis=0))


def band_ones():
    width = BAND // 4
    first = lax.broadcasted_iota(jnp.int32, (GROUP, GROUP), 0) // width
    second = lax.broadcasted_iota(jnp.int32, (GROUP, GROUP), 1) // width
    return jnp.where(first == second, 1.0, 0.0).astype(jnp.bfloat16)


def split(x):
    high = x.astype(jnp.bfloat16)
    low = (x - high.astype(jnp.float32)).astype(jnp.bfloat16)
    return high, low


def mxu(a, b):
    return jnp.dot(a, b, preferred_element_type=jnp.float32)


def rounded(v):
    return v.astype(jnp.bfloat16).astype(jnp.float32)


def groups(v):
    return [v[:, c : c + GROUP] for c in range(0, v.shape[1], GROUP)]


def wide_mxu(v, table, rows, cols):
    high, low = split(v)
    count = v.shape[0]
    first = mxu(jnp.concatenate([high, low], axis=0), table[0, rows, cols])
    return first[:count] + first[count:] + mxu(high, table[1, rows, cols])


EVEN, ODD = slice(0, QUARTER), slice(QUARTER, 3 * QUARTER)
LEFT, RIGHT, ALL = slice(0, QUARTER), slice(QUARTER, 2 * QUARTER), slice(None)


def spectrum(x, table):
    q = [x[:, c : c + QUARTER] for c in range(0, SEG_LEN, QUARTER)]
    plus, cross = q[0] + q[2], q[1] + q[3]
    zero = wide_mxu(plus + cross, table, EVEN, LEFT)
    two = wide_mxu(plus - cross, table, EVEN, RIGHT)
    odd = wide_mxu(
        jnp.concatenate([q[0] - q[2], q[1] - q[3]], axis=1), table, ODD, ALL)
    real = [zero[:, :GROUP], two[:, :GROUP], odd[:, : 2 * GROUP]]
    imag = [zero[:, GROUP:], two[:, GROUP:], odd[:, 2 * GROUP :]]
    return jnp.concatenate(real + imag, axis=1)


def lags_of(v, table):
    g = groups(v)
    zero = wide_mxu(jnp.concatenate([g[0], g[4]], axis=1), table, EVEN, LEFT)
    two = wide_mxu(jnp.concatenate([g[1], g[5]], axis=1), table, EVEN, RIGHT)
    odd = wide_mxu(
        jnp.concatenate([g[2], g[3], g[6], g[7]], axis=1), table, ODD, ALL)
    return jnp.concatenate([zero + two, zero - two], axis=1) + odd


def kernel(
    nblk, nsub, wide,
    raw, valid, choose, dft, lag, out,
    select, part, own, vpart, vown, x32, vcol, dft_v, lag_v,
    send, recv, vsend, vrecv, fsend, frecv, local, tabs,
):
    me_b, me_u = lax.axis_index("blk"), lax.axis_index("sub")
    rows = wide * nsub
    prow = wide * nblk
    blks, subs = range(1, nblk), range(1, nsub)

    def at_blk(db):
        return {"blk": lax.rem(me_b + db, nblk)}

    def at_sub(du):
        return {"sub": lax.rem(me_u + du, nsub)}

    tab_copies = [
        pltpu.make_async_copy(dft, dft_v, tabs.at[0]),
        pltpu.make_async_copy(lag, lag_v, tabs.at[1]),
    ]
    mine = [
        pltpu.make_async_copy(raw, part.at[0], local.at[0]),
        pltpu.make_async_copy(valid, vpart.at[me_b], local.at[1]),
        pltpu.make_async_copy(valid, vown.at[me_u], local.at[2]),
        pltpu.make_async_copy(choose, select, local.at[3]),
        pltpu.make_async_copy(raw.at[me_b], own.at[0, me_u], local.at[4]),
    ]

    barrier = pltpu.get_barrier_semaphore()
    order = list(blks)
    others = [(db, du) for db in range(nblk) for du in range(nsub) if db or du]
    for db, du in others:
        pl.semaphore_signal(
            barrier, inc=1, device_id={**at_blk(db), **at_sub(du)}, device_id_type=MESH)
    for copy in mine:
        copy.start()
    pl.semaphore_wait(barrier, len(others))

    def samples(db):
        return pltpu.make_async_remote_copy(
            raw, part.at[db], send.at[db], recv.at[db],
            device_id=at_blk(db), device_id_type=MESH)

    def valid_blk(db, at_b):
        return pltpu.make_async_remote_copy(
            valid, vpart.at[at_b], vsend.at[db], vrecv.at[db],
            device_id=at_blk(db), device_id_type=MESH)

    def valid_sub(du, at_u):
        return pltpu.make_async_remote_copy(
            valid, vown.at[at_u], vsend.at[nblk + du], vrecv.at[nblk + du],
            device_id=at_sub(du), device_id_type=MESH)

    def block(db, du, at_u):
        there = at_blk(db)
        return pltpu.make_async_remote_copy(
            raw.at[there["blk"]], own.at[db, at_u], fsend.at[db, du], frecv.at[db, du],
            device_id={**there, **at_sub(du)}, device_id_type=MESH)

    sent = [samples(db) for db in order]
    sent += [valid_blk(db, me_b) for db in order]
    sent += [valid_sub(du, me_u) for du in subs]
    sent += [block(db, du, me_u) for db in range(nblk) for du in subs]
    for copy in sent + tab_copies:
        copy.start()

    def place(ref, base, count):
        for c in range(count):
            x32[pl.ds(base + c * wide, wide), :] = ref[c].astype(jnp.float32)

    base = nblk * prow
    for copy in mine:
        copy.wait()
    place(part.at[0], 0, nblk)
    moved = []
    for db in order:
        samples(db).wait_recv()
        keep = pltpu.make_async_copy(
            part.at[db, me_b], own.at[db, me_u], fsend.at[db, 0])
        keep.start()
        moved.append(keep)
        place(part.at[db], db * prow, nblk)

    for db in blks:
        valid_blk(db, lax.rem(me_b + nblk - db, nblk)).wait_recv()
    for du in subs:
        valid_sub(du, lax.rem(me_u + nsub - du, nsub)).wait_recv()
    for n in range(nblk):
        for k in range(wide):
            vcol[pl.ds(n * wide + k, 1), :] = jnp.broadcast_to(
                vpart[n][:, k : k + 1].astype(jnp.float32), (1, 128))
    for u in range(nsub):
        for k in range(wide):
            vcol[pl.ds(prow + u * wide + k, 1), :] = jnp.broadcast_to(
                vown[u][:, k : k + 1].astype(jnp.float32), (1, 128))

    tab_copies[0].wait()
    for copy in moved:
        copy.wait()
    for db in [0] + order:
        for du in subs:
            block(db, du, lax.rem(me_u + nsub - du, nsub)).wait_recv()
        place(own.at[db], base + db * rows, nsub)
    spec = spectrum(x32[...], dft_v)
    power = sum(g * g for g in groups(spec))
    sums = [power[c : c + prow] for c in range(0, base, prow)]
    part_sum = functools.reduce(jnp.add, sums)
    sums = [power[c : c + rows] for c in range(base, base + nblk * rows, rows)]
    own_sum = functools.reduce(jnp.add, sums)
    high, low = split(jnp.concatenate([part_sum, own_sum], axis=0))
    total = mxu(jnp.concatenate([high, low], axis=0), band_ones())
    level = (total[: prow + rows] + total[prow + rows :]) * (1.0 / (BAND * nblk))
    factor = jnp.tile(lax.rsqrt(level + eps) * vcol[...], (1, 8))
    row_id = lax.broadcasted_iota(jnp.int32, (prow, 1), 0) // wide
    partner = []
    for db in range(nblk):
        w = jnp.zeros((prow, 1), jnp.float32)
        seg = lax.rem(me_b + nblk - db, nblk)
        for n in range(nblk):
            w = jnp.where(row_id == n, select[0, n, seg].astype(jnp.float32), w)
        partner.append(rounded(spec[db * prow : (db + 1) * prow] * factor[:prow]) * w)

    acc_re = [0.0] * rows
    acc_im = [0.0] * rows
    for db in range(nblk):
        first = base + db * rows
        a = rounded(spec[first : first + rows] * factor[prow:])
        br, bi = partner[db][:, :BINS], partner[db][:, BINS:]
        for i in range(rows):
            ar, ai = a[i : i + 1, :BINS], a[i : i + 1, BINS:]
            acc_re[i] = acc_re[i] + (ar * br + ai * bi)
            acc_im[i] = acc_im[i] + (ai * br - ar * bi)
    stacked = jnp.concatenate(
        [jnp.concatenate(acc_re, axis=0), jnp.concatenate(acc_im, axis=0)], axis=1)
    tab_copies[1].wait()
    out[...] = lags_of(stacked, lag_v)
    for copy in sent:
        copy.wait_send()


def fused(nblk, nsub, raw, valid, select):
    wide = raw.shape[1]
    rows, prow = wide * nsub, wide * nblk
    tables = (
        jnp.asarray(dft_split()),
        jnp.asarray(lag_split(1.0 / math.sqrt(BINS * nblk))),
    )
    hbm = pl.BlockSpec(memory_space=pltpu.HBM)
    result = pl.pallas_call(
        functools.partial(kernel, nblk, nsub, wide),
        out_shape=jax.ShapeDtypeStruct((rows * prow, LAGS), jnp.float32),
        in_specs=[hbm] * 5,
        out_specs=pl.BlockSpec(memory_space=pltpu.VMEM),
        scratch_shapes=[
            pltpu.SMEM(select.shape, jnp.int32),
            pltpu.VMEM((nblk, nblk, wide, SEG_LEN), jnp.bfloat16),
            pltpu.VMEM((nblk, nsub, wide, SEG_LEN), jnp.bfloat16),
            pltpu.VMEM((nblk, 1, wide), jnp.int32),
            pltpu.VMEM((nsub, 1, wide), jnp.int32),
            pltpu.VMEM((nblk * (rows + prow), SEG_LEN), jnp.float32),
            pltpu.VMEM((rows + prow, 128), jnp.float32),
            pltpu.VMEM((2, 3 * QUARTER, BINS), jnp.bfloat16),
            pltpu.VMEM((2, 3 * QUARTER, LAGS), jnp.bfloat16),
            pltpu.SemaphoreType.DMA((nblk,)),
            pltpu.SemaphoreType.DMA((nblk,)),
            pltpu.SemaphoreType.DMA((nblk + nsub,)),
            pltpu.SemaphoreType.DMA((nblk + nsub,)),
            pltpu.SemaphoreType.DMA((nblk, nsub)),
            pltpu.SemaphoreType.DMA((nblk, nsub)),
            pltpu.SemaphoreType.DMA((5,)),
            pltpu.SemaphoreType.DMA((2,)),
        ],
        compiler_params=pltpu.CompilerParams(
            collective_id=0, has_side_effects=True, vmem_limit_bytes=32 * 2**20
        ),
    )(*(pltpu.with_memory_space_constraint(a, pltpu.HBM) for a in (raw, valid, select) + tables))
    return result.reshape(rows, nblk, wide, LAGS)


def dft_tables(length, bins):
    times = jnp.arange(length, dtype=jnp.int32)[:, None]
    freqs = jnp.arange(bins, dtype=jnp.int32)[None, :]
    angle = (times * freqs % length).astype(jnp.float32) * (2.0 * math.pi / length)
    return (jnp.cos(angle), -jnp.sin(angle))


def whiten(records, valid, seg_len, band):
    chans = records.shape[0] * records.shape[1]
    frames = records.astype(jnp.float32).reshape(chans, -1, seg_len)
    segs = frames.shape[1]
    bins = seg_len // 2
    cos_tab, sin_tab = dft_tables(seg_len, bins)
    real = jnp.einsum("cst,tf->csf", frames, cos_tab, precision=lax.Precision.HIGHEST)
    imag = jnp.einsum("cst,tf->csf", frames, sin_tab, precision=lax.Precision.HIGHEST)
    bands = bins // band
    power = (real * real + imag * imag).reshape(chans, segs, bands, band)
    level = jnp.mean(power, axis=(1, 3))
    factor = valid.reshape(chans, 1).astype(jnp.float32) / jnp.sqrt(level + eps)
    factor = factor[:, None, :, None]
    real = (real.reshape(chans, segs, bands, band) * factor).reshape(chans, segs, bins)
    imag = (imag.reshape(chans, segs, bands, band) * factor).reshape(chans, segs, bins)
    return jnp.stack([real, imag], axis=2).astype(jnp.bfloat16)


def lag_table(bins, lags, seg_len, scale):
    freqs = jnp.arange(bins, dtype=jnp.int32)[:, None]
    shifts = jnp.arange(lags, dtype=jnp.int32)[None, :] - lags // 2
    angle = (freqs * shifts % seg_len).astype(jnp.float32) * (2.0 * math.pi / seg_len)
    weight = jnp.where(freqs == 0, 1.0, 2.0).astype(jnp.float32) * scale
    return jnp.stack([weight * jnp.cos(angle), -weight * jnp.sin(angle)])


def pair_terms(own, weight_rows, piece):
    masked = piece * weight_rows.astype(jnp.bfloat16)[:, None, :, None, None]
    prod = jnp.einsum("isaf,njsbf->injabf", own, masked, preferred_element_type=jnp.float32)
    real = prod[:, :, :, 0, 0] + prod[:, :, :, 1, 1]
    imag = prod[:, :, :, 1, 0] - prod[:, :, :, 0, 1]
    return jnp.stack([real, imag], axis=3)


def by_collectives(raw, valid, select):
    regrouped = lax.all_to_all(raw, "blk", split_axis=0, concat_axis=2, tiled=True)
    spectra = whiten(regrouped, valid, SEG_LEN, BAND)
    segs = spectra.shape[1]
    table = lag_table(BINS, LAGS, SEG_LEN, 1.0 / math.sqrt(BINS * segs))
    block = lax.all_gather(spectra, "sub", axis=0, tiled=True)
    stacked = pair_terms(
        block, select[0], lax.all_gather(spectra[None], "blk", axis=0, tiled=True)
    )
    return jnp.einsum("injrf,rfl->injl", stacked, table, precision=lax.Precision.HIGHEST)


def solution(mesh):
    nblk, nsub = mesh.shape["blk"], mesh.shape["sub"]

    def per_device(raw, valid, select):
        fits = raw.shape[2] == SEG_LEN and raw.shape[0] == nblk and nblk * nsub <= 16
        if fits:
            return fused(nblk, nsub, raw, valid, select)
        return by_collectives(raw, valid, select)

    return jax.shard_map(
        per_device,
        mesh=mesh,
        in_specs=(
            P("cable", "sub", "blk"),
            P(("cable", "blk"), "sub"),
            P(("cable", "blk"), None, None),
        ),
        out_specs=P(("cable", "blk"), None, "sub", None),
        check_vma=False,
    )
```

```python
import functools
import math

import jax
import jax.numpy as jnp
import numpy as np
from jax import lax
from jax.experimental import pallas as pl
from jax.experimental.pallas import tpu as pltpu
from jax.sharding import PartitionSpec as P

SEG_LEN = 1024
BAND = 64
LAGS = 512
BINS = SEG_LEN // 2
QUARTER = SEG_LEN // 4
GROUP = BINS // 4

eps = 1e-06
MESH = pl.DeviceIdType.MESH


def split_table(table):
    high = table.astype(np.float32).astype(jnp.bfloat16)
    low = (table - high.astype(np.float64)).astype(np.float32).astype(jnp.bfloat16)
    return np.stack([high, low])


def waves(freqs, times):
    angle = (freqs * times % SEG_LEN) * (2.0 * math.pi / SEG_LEN)
    return np.cos(angle), -np.sin(angle)


def bins_of(*classes):
    return np.concatenate([np.arange(r, BINS, 4) for r in classes])


def dft_split():
    def table(length, *classes):
        freqs = bins_of(*classes)[None, :]
        return np.concatenate(waves(freqs, np.arange(length)[:, None]), axis=1)

    even = np.concatenate([table(QUARTER, 0), table(QUARTER, 2)], axis=1)
    return split_table(np.concatenate([even, table(2 * QUARTER, 1, 3)], axis=0))


def lag_split(scale):
    def table(count, *classes):
        freqs = bins_of(*classes)[:, None]
        weight = np.where(freqs == 0, 1.0, 2.0) * scale
        shifts = np.arange(count)[None, :] - LAGS // 2
        return np.concatenate([weight * w for w in waves(freqs, shifts)], axis=0)

    even = np.concatenate([table(LAGS // 2, 0), table(LAGS // 2, 2)], axis=1)
    return split_table(np.concatenate([even, table(LAGS, 1, 3)], axis=0))


def band_ones():
    width = BAND // 4
    first = lax.broadcasted_iota(jnp.int32, (GROUP, GROUP), 0) // width
    second = lax.broadcasted_iota(jnp.int32, (GROUP, GROUP), 1) // width
    return jnp.where(first == second, 1.0, 0.0).astype(jnp.bfloat16)


def split(x):
    high = x.astype(jnp.bfloat16)
    low = (x - high.astype(jnp.float32)).astype(jnp.bfloat16)
    return high, low


def mxu(a, b):
    return jnp.dot(a, b, preferred_element_type=jnp.float32)


def rounded(v):
    return v.astype(jnp.bfloat16).astype(jnp.float32)


def groups(v):
    return [v[:, c : c + GROUP] for c in range(0, v.shape[1], GROUP)]


def wide_mxu(v, table, rows, cols):
    high, low = split(v)
    count = v.shape[0]
    first = mxu(jnp.concatenate([high, low], axis=0), table[0, rows, cols])
    return first[:count] + first[count:] + mxu(high, table[1, rows, cols])


EVEN, ODD = slice(0, QUARTER), slice(QUARTER, 3 * QUARTER)
LEFT, RIGHT, ALL = slice(0, QUARTER), slice(QUARTER, 2 * QUARTER), slice(None)


def spectrum(x, table):
    q = [x[:, c : c + QUARTER] for c in range(0, SEG_LEN, QUARTER)]
    plus, cross = q[0] + q[2], q[1] + q[3]
    zero = wide_mxu(plus + cross, table, EVEN, LEFT)
    two = wide_mxu(plus - cross, table, EVEN, RIGHT)
    odd = wide_mxu(
        jnp.concatenate([q[0] - q[2], q[1] - q[3]], axis=1), table, ODD, ALL)
    real = [zero[:, :GROUP], two[:, :GROUP], odd[:, : 2 * GROUP]]
    imag = [zero[:, GROUP:], two[:, GROUP:], odd[:, 2 * GROUP :]]
    return jnp.concatenate(real + imag, axis=1)


def lags_of(v, table):
    g = groups(v)
    zero = wide_mxu(jnp.concatenate([g[0], g[4]], axis=1), table, EVEN, LEFT)
    two = wide_mxu(jnp.concatenate([g[1], g[5]], axis=1), table, EVEN, RIGHT)
    odd = wide_mxu(
        jnp.concatenate([g[2], g[3], g[6], g[7]], axis=1), table, ODD, ALL)
    return jnp.concatenate([zero + two, zero - two], axis=1) + odd


def kernel(
    nblk, nsub, wide,
    raw, valid, choose, dft, lag, out,
    select, part, own, vpart, vown, x32, vcol, dft_v, lag_v,
    send, recv, vsend, vrecv, fsend, frecv, local, tabs,
):
    me_b, me_u = lax.axis_index("blk"), lax.axis_index("sub")
    rows = wide * nsub
    prow = wide * nblk
    blks, subs = range(1, nblk), range(1, nsub)

    def at_blk(db):
        return {"blk": lax.rem(me_b + db, nblk)}

    def at_sub(du):
        return {"sub": lax.rem(me_u + du, nsub)}

    tab_copies = [
        pltpu.make_async_copy(dft, dft_v, tabs.at[0]),
        pltpu.make_async_copy(lag, lag_v, tabs.at[1]),
    ]
    mine = [
        pltpu.make_async_copy(raw, part.at[0], local.at[0]),
        pltpu.make_async_copy(valid, vpart.at[me_b], local.at[1]),
        pltpu.make_async_copy(valid, vown.at[me_u], local.at[2]),
        pltpu.make_async_copy(choose, select, local.at[3]),
        pltpu.make_async_copy(raw.at[me_b], own.at[0, me_u], local.at[4]),
    ]

    barrier = pltpu.get_barrier_semaphore()
    order = list(blks)
    others = [(db, du) for db in range(nblk) for du in range(nsub) if db or du]
    for db, du in others:
        pl.semaphore_signal(
            barrier, inc=1, device_id={**at_blk(db), **at_sub(du)}, device_id_type=MESH)
    for copy in mine:
        copy.start()
    pl.semaphore_wait(barrier, len(others))

    def samples(db):
        return pltpu.make_async_remote_copy(
            part.at[0], part.at[db], send.at[db], recv.at[db],
            device_id=at_blk(db), device_id_type=MESH)

    def valid_blk(db, at_b):
        return pltpu.make_async_remote_copy(
            valid, vpart.at[at_b], vsend.at[db], vrecv.at[db],
            device_id=at_blk(db), device_id_type=MESH)

    def valid_sub(du, at_u):
        return pltpu.make_async_remote_copy(
            valid, vown.at[at_u], vsend.at[nblk + du], vrecv.at[nblk + du],
            device_id=at_sub(du), device_id_type=MESH)

    def block(db, du, at_u):
        there = at_blk(db)
        return pltpu.make_async_remote_copy(
            part.at[0, there["blk"]], own.at[db, at_u], fsend.at[db, du], frecv.at[db, du],
            device_id={**there, **at_sub(du)}, device_id_type=MESH)

    for copy in mine:
        copy.wait()
    sent = [samples(db) for db in order]
    sent += [valid_blk(db, me_b) for db in order]
    sent += [valid_sub(du, me_u) for du in subs]
    sent += [block(db, du, me_u) for db in order for du in subs]
    sent += [block(0, du, me_u) for du in subs]
    for copy in sent + tab_copies:
        copy.start()

    def place(ref, base, count):
        for c in range(count):
            x32[pl.ds(base + c * wide, wide), :] = ref[c].astype(jnp.float32)

    base = nblk * prow
    place(part.at[0], 0, nblk)
    moved = []
    for db in order:
        samples(db).wait_recv()
        keep = pltpu.make_async_copy(
            part.at[db, me_b], own.at[db, me_u], fsend.at[db, 0])
        keep.start()
        moved.append(keep)
        place(part.at[db], db * prow, nblk)

    for db in blks:
        valid_blk(db, lax.rem(me_b + nblk - db, nblk)).wait_recv()
    for du in subs:
        valid_sub(du, lax.rem(me_u + nsub - du, nsub)).wait_recv()
    for n in range(nblk):
        for k in range(wide):
            vcol[pl.ds(n * wide + k, 1), :] = jnp.broadcast_to(
                vpart[n][:, k : k + 1].astype(jnp.float32), (1, 128))
    for u in range(nsub):
        for k in range(wide):
            vcol[pl.ds(prow + u * wide + k, 1), :] = jnp.broadcast_to(
                vown[u][:, k : k + 1].astype(jnp.float32), (1, 128))

    tab_copies[0].wait()
    for copy in moved:
        copy.wait()
    for db in [0] + order:
        for du in subs:
            block(db, du, lax.rem(me_u + nsub - du, nsub)).wait_recv()
        place(own.at[db], base + db * rows, nsub)
    spec = spectrum(x32[...], dft_v)
    power = sum(g * g for g in groups(spec))
    sums = [power[c : c + prow] for c in range(0, base, prow)]
    part_sum = functools.reduce(jnp.add, sums)
    sums = [power[c : c + rows] for c in range(base, base + nblk * rows, rows)]
    own_sum = functools.reduce(jnp.add, sums)
    high, low = split(jnp.concatenate([part_sum, own_sum], axis=0))
    total = mxu(jnp.concatenate([high, low], axis=0), band_ones())
    level = (total[: prow + rows] + total[prow + rows :]) * (1.0 / (BAND * nblk))
    factor = jnp.tile(lax.rsqrt(level + eps) * vcol[...], (1, 8))
    row_id = lax.broadcasted_iota(jnp.int32, (prow, 1), 0) // wide
    partner = []
    for db in range(nblk):
        w = jnp.zeros((prow, 1), jnp.float32)
        seg = lax.rem(me_b + nblk - db, nblk)
        for n in range(nblk):
            w = jnp.where(row_id == n, select[0, n, seg].astype(jnp.float32), w)
        partner.append(rounded(spec[db * prow : (db + 1) * prow] * factor[:prow]) * w)

    acc_re = [0.0] * rows
    acc_im = [0.0] * rows
    for db in range(nblk):
        first = base + db * rows
        a = rounded(spec[first : first + rows] * factor[prow:])
        br, bi = partner[db][:, :BINS], partner[db][:, BINS:]
        for i in range(rows):
            ar, ai = a[i : i + 1, :BINS], a[i : i + 1, BINS:]
            acc_re[i] = acc_re[i] + (ar * br + ai * bi)
            acc_im[i] = acc_im[i] + (ai * br - ar * bi)
    stacked = jnp.concatenate(
        [jnp.concatenate(acc_re, axis=0), jnp.concatenate(acc_im, axis=0)], axis=1)
    tab_copies[1].wait()
    out[...] = lags_of(stacked, lag_v)
    for copy in sent:
        copy.wait_send()


def fused(nblk, nsub, raw, valid, select):
    wide = raw.shape[1]
    rows, prow = wide * nsub, wide * nblk
    tables = (
        jnp.asarray(dft_split()),
        jnp.asarray(lag_split(1.0 / math.sqrt(BINS * nblk))),
    )
    hbm = pl.BlockSpec(memory_space=pltpu.HBM)
    result = pl.pallas_call(
        functools.partial(kernel, nblk, nsub, wide),
        out_shape=jax.ShapeDtypeStruct((rows * prow, LAGS), jnp.float32),
        in_specs=[hbm] * 5,
        out_specs=pl.BlockSpec(memory_space=pltpu.VMEM),
        scratch_shapes=[
            pltpu.SMEM(select.shape, jnp.int32),
            pltpu.VMEM((nblk, nblk, wide, SEG_LEN), jnp.bfloat16),
            pltpu.VMEM((nblk, nsub, wide, SEG_LEN), jnp.bfloat16),
            pltpu.VMEM((nblk, 1, wide), jnp.int32),
            pltpu.VMEM((nsub, 1, wide), jnp.int32),
            pltpu.VMEM((nblk * (rows + prow), SEG_LEN), jnp.float32),
            pltpu.VMEM((rows + prow, 128), jnp.float32),
            pltpu.VMEM((2, 3 * QUARTER, BINS), jnp.bfloat16),
            pltpu.VMEM((2, 3 * QUARTER, LAGS), jnp.bfloat16),
            pltpu.SemaphoreType.DMA((nblk,)),
            pltpu.SemaphoreType.DMA((nblk,)),
            pltpu.SemaphoreType.DMA((nblk + nsub,)),
            pltpu.SemaphoreType.DMA((nblk + nsub,)),
            pltpu.SemaphoreType.DMA((nblk, nsub)),
            pltpu.SemaphoreType.DMA((nblk, nsub)),
            pltpu.SemaphoreType.DMA((5,)),
            pltpu.SemaphoreType.DMA((2,)),
        ],
        compiler_params=pltpu.CompilerParams(
            collective_id=0, has_side_effects=True, vmem_limit_bytes=32 * 2**20
        ),
    )(*(pltpu.with_memory_space_constraint(a, pltpu.HBM) for a in (raw, valid, select) + tables))
    return result.reshape(rows, nblk, wide, LAGS)


def dft_tables(length, bins):
    times = jnp.arange(length, dtype=jnp.int32)[:, None]
    freqs = jnp.arange(bins, dtype=jnp.int32)[None, :]
    angle = (times * freqs % length).astype(jnp.float32) * (2.0 * math.pi / length)
    return (jnp.cos(angle), -jnp.sin(angle))


def whiten(records, valid, seg_len, band):
    chans = records.shape[0] * records.shape[1]
    frames = records.astype(jnp.float32).reshape(chans, -1, seg_len)
    segs = frames.shape[1]
    bins = seg_len // 2
    cos_tab, sin_tab = dft_tables(seg_len, bins)
    real = jnp.einsum("cst,tf->csf", frames, cos_tab, precision=lax.Precision.HIGHEST)
    imag = jnp.einsum("cst,tf->csf", frames, sin_tab, precision=lax.Precision.HIGHEST)
    bands = bins // band
    power = (real * real + imag * imag).reshape(chans, segs, bands, band)
    level = jnp.mean(power, axis=(1, 3))
    factor = valid.reshape(chans, 1).astype(jnp.float32) / jnp.sqrt(level + eps)
    factor = factor[:, None, :, None]
    real = (real.reshape(chans, segs, bands, band) * factor).reshape(chans, segs, bins)
    imag = (imag.reshape(chans, segs, bands, band) * factor).reshape(chans, segs, bins)
    return jnp.stack([real, imag], axis=2).astype(jnp.bfloat16)


def lag_table(bins, lags, seg_len, scale):
    freqs = jnp.arange(bins, dtype=jnp.int32)[:, None]
    shifts = jnp.arange(lags, dtype=jnp.int32)[None, :] - lags // 2
    angle = (freqs * shifts % seg_len).astype(jnp.float32) * (2.0 * math.pi / seg_len)
    weight = jnp.where(freqs == 0, 1.0, 2.0).astype(jnp.float32) * scale
    return jnp.stack([weight * jnp.cos(angle), -weight * jnp.sin(angle)])


def pair_terms(own, weight_rows, piece):
    masked = piece * weight_rows.astype(jnp.bfloat16)[:, None, :, None, None]
    prod = jnp.einsum("isaf,njsbf->injabf", own, masked, preferred_element_type=jnp.float32)
    real = prod[:, :, :, 0, 0] + prod[:, :, :, 1, 1]
    imag = prod[:, :, :, 1, 0] - prod[:, :, :, 0, 1]
    return jnp.stack([real, imag], axis=3)


def by_collectives(raw, valid, select):
    regrouped = lax.all_to_all(raw, "blk", split_axis=0, concat_axis=2, tiled=True)
    spectra = whiten(regrouped, valid, SEG_LEN, BAND)
    segs = spectra.shape[1]
    table = lag_table(BINS, LAGS, SEG_LEN, 1.0 / math.sqrt(BINS * segs))
    block = lax.all_gather(spectra, "sub", axis=0, tiled=True)
    stacked = pair_terms(
        block, select[0], lax.all_gather(spectra[None], "blk", axis=0, tiled=True)
    )
    return jnp.einsum("injrf,rfl->injl", stacked, table, precision=lax.Precision.HIGHEST)


def solution(mesh):
    nblk, nsub = mesh.shape["blk"], mesh.shape["sub"]

    def per_device(raw, valid, select):
        fits = raw.shape[2] == SEG_LEN and raw.shape[0] == nblk and nblk * nsub <= 16
        if fits:
            return fused(nblk, nsub, raw, valid, select)
        return by_collectives(raw, valid, select)

    return jax.shard_map(
        per_device,
        mesh=mesh,
        in_specs=(
            P("cable", "sub", "blk"),
            P(("cable", "blk"), "sub"),
            P(("cable", "blk"), None, None),
        ),
        out_specs=P(("cable", "blk"), None, "sub", None),
        check_vma=False,
    )
```

```python
import functools
import math

import jax
import jax.numpy as jnp
import numpy as np
from jax import lax
from jax.experimental import pallas as pl
from jax.experimental.pallas import tpu as pltpu
from jax.sharding import PartitionSpec as P

SEG_LEN = 1024
BAND = 64
LAGS = 512
BINS = SEG_LEN // 2
QUARTER = SEG_LEN // 4
GROUP = BINS // 4

eps = 1e-06
MESH = pl.DeviceIdType.MESH


def split_table(table):
    high = table.astype(np.float32).astype(jnp.bfloat16)
    low = (table - high.astype(np.float64)).astype(np.float32).astype(jnp.bfloat16)
    return np.stack([high, low])


def waves(freqs, times):
    angle = (freqs * times % SEG_LEN) * (2.0 * math.pi / SEG_LEN)
    return np.cos(angle), -np.sin(angle)


def bins_of(*classes):
    return np.concatenate([np.arange(r, BINS, 4) for r in classes])


def dft_split():
    def table(length, *classes):
        freqs = bins_of(*classes)[None, :]
        return np.concatenate(waves(freqs, np.arange(length)[:, None]), axis=1)

    even = np.concatenate([table(QUARTER, 0), table(QUARTER, 2)], axis=1)
    return split_table(np.concatenate([even, table(2 * QUARTER, 1, 3)], axis=0))


def lag_split(scale):
    def table(count, *classes):
        freqs = bins_of(*classes)[:, None]
        weight = np.where(freqs == 0, 1.0, 2.0) * scale
        shifts = np.arange(count)[None, :] - LAGS // 2
        return np.concatenate([weight * w for w in waves(freqs, shifts)], axis=0)

    even = np.concatenate([table(LAGS // 2, 0), table(LAGS // 2, 2)], axis=1)
    return split_table(np.concatenate([even, table(LAGS, 1, 3)], axis=0))


def band_ones():
    width = BAND // 4
    first = lax.broadcasted_iota(jnp.int32, (GROUP, GROUP), 0) // width
    second = lax.broadcasted_iota(jnp.int32, (GROUP, GROUP), 1) // width
    return jnp.where(first == second, 1.0, 0.0).astype(jnp.bfloat16)


def split(x):
    high = x.astype(jnp.bfloat16)
    low = (x - high.astype(jnp.float32)).astype(jnp.bfloat16)
    return high, low


def mxu(a, b):
    return jnp.dot(a, b, preferred_element_type=jnp.float32)


def rounded(v):
    return v.astype(jnp.bfloat16).astype(jnp.float32)


def groups(v):
    return [v[:, c : c + GROUP] for c in range(0, v.shape[1], GROUP)]


def wide_mxu(v, table, rows, cols):
    high, low = split(v)
    count = v.shape[0]
    first = mxu(jnp.concatenate([high, low], axis=0), table[0, rows, cols])
    return first[:count] + first[count:] + mxu(high, table[1, rows, cols])


EVEN, ODD = slice(0, QUARTER), slice(QUARTER, 3 * QUARTER)
LEFT, RIGHT, ALL = slice(0, QUARTER), slice(QUARTER, 2 * QUARTER), slice(None)


def spectrum(x, table):
    q = [x[:, c : c + QUARTER] for c in range(0, SEG_LEN, QUARTER)]
    plus, cross = q[0] + q[2], q[1] + q[3]
    zero = wide_mxu(plus + cross, table, EVEN, LEFT)
    two = wide_mxu(plus - cross, table, EVEN, RIGHT)
    odd = wide_mxu(
        jnp.concatenate([q[0] - q[2], q[1] - q[3]], axis=1), table, ODD, ALL)
    real = [zero[:, :GROUP], two[:, :GROUP], odd[:, : 2 * GROUP]]
    imag = [zero[:, GROUP:], two[:, GROUP:], odd[:, 2 * GROUP :]]
    return jnp.concatenate(real + imag, axis=1)


def lags_of(v, table):
    g = groups(v)
    zero = wide_mxu(jnp.concatenate([g[0], g[4]], axis=1), table, EVEN, LEFT)
    two = wide_mxu(jnp.concatenate([g[1], g[5]], axis=1), table, EVEN, RIGHT)
    odd = wide_mxu(
        jnp.concatenate([g[2], g[3], g[6], g[7]], axis=1), table, ODD, ALL)
    return jnp.concatenate([zero + two, zero - two], axis=1) + odd


def kernel(
    nblk, nsub, wide,
    raw, valid, choose, dft, lag, out,
    select, part, own, vpart, vown, x32, vcol, dft_v, lag_v,
    send, recv, vsend, vrecv, fsend, frecv, local, tabs,
):
    me_b, me_u = lax.axis_index("blk"), lax.axis_index("sub")
    rows = wide * nsub
    prow = wide * nblk
    blks, subs = range(1, nblk), range(1, nsub)

    def at_blk(db):
        return {"blk": lax.rem(me_b + db, nblk)}

    def at_sub(du):
        return {"sub": lax.rem(me_u + du, nsub)}

    tab_copies = [
        pltpu.make_async_copy(dft, dft_v, tabs.at[0]),
        pltpu.make_async_copy(lag, lag_v, tabs.at[1]),
    ]
    mine = [
        pltpu.make_async_copy(raw, part.at[0], local.at[0]),
        pltpu.make_async_copy(valid, vpart.at[me_b], local.at[1]),
        pltpu.make_async_copy(valid, vown.at[me_u], local.at[2]),
        pltpu.make_async_copy(choose, select, local.at[3]),
        pltpu.make_async_copy(raw.at[me_b], own.at[0, me_u], local.at[4]),
    ]

    barrier = pltpu.get_barrier_semaphore()
    order = list(blks)
    others = [(db, du) for db in range(nblk) for du in range(nsub) if db or du]
    for db, du in others:
        pl.semaphore_signal(
            barrier, inc=1, device_id={**at_blk(db), **at_sub(du)}, device_id_type=MESH)
    for copy in mine:
        copy.start()
    pl.semaphore_wait(barrier, len(others))

    def samples(db):
        return pltpu.make_async_remote_copy(
            part.at[0], part.at[db], send.at[db], recv.at[db],
            device_id=at_blk(db), device_id_type=MESH)

    def valid_blk(db, at_b):
        return pltpu.make_async_remote_copy(
            valid, vpart.at[at_b], vsend.at[db], vrecv.at[db],
            device_id=at_blk(db), device_id_type=MESH)

    def valid_sub(du, at_u):
        return pltpu.make_async_remote_copy(
            valid, vown.at[at_u], vsend.at[nblk + du], vrecv.at[nblk + du],
            device_id=at_sub(du), device_id_type=MESH)

    def block(db, du, at_u):
        there = at_blk(db)
        return pltpu.make_async_remote_copy(
            part.at[0, there["blk"]], own.at[db, at_u], fsend.at[db, du], frecv.at[db, du],
            device_id={**there, **at_sub(du)}, device_id_type=MESH)

    for copy in mine:
        copy.wait()
    sent = [samples(db) for db in order]
    sent += [valid_blk(db, me_b) for db in order]
    sent += [valid_sub(du, me_u) for du in subs]
    sent += [block(db, du, me_u) for db in order for du in subs]
    sent += [block(0, du, me_u) for du in subs]
    for copy in sent + tab_copies:
        copy.start()

    def place(ref, base, count):
        for c in range(count):
            x32[pl.ds(base + c * wide, wide), :] = ref[c].astype(jnp.float32)

    base = nblk * prow
    place(part.at[0], 0, nblk)
    moved = []
    for db in order:
        samples(db).wait_recv()
        keep = pltpu.make_async_copy(
            part.at[db, me_b], own.at[db, me_u], fsend.at[db, 0])
        keep.start()
        moved.append(keep)
        place(part.at[db], db * prow, nblk)

    for db in blks:
        valid_blk(db, lax.rem(me_b + nblk - db, nblk)).wait_recv()
    for du in subs:
        valid_sub(du, lax.rem(me_u + nsub - du, nsub)).wait_recv()
    for n in range(nblk):
        for k in range(wide):
            vcol[pl.ds(n * wide + k, 1), :] = jnp.broadcast_to(
                vpart[n][:, k : k + 1].astype(jnp.float32), (1, 128))
    for u in range(nsub):
        for k in range(wide):
            vcol[pl.ds(prow + u * wide + k, 1), :] = jnp.broadcast_to(
                vown[u][:, k : k + 1].astype(jnp.float32), (1, 128))

    tab_copies[0].wait()
    tab_copies[1].wait()
    for copy in moved:
        copy.wait()
    for db in [0] + order:
        for du in subs:
            block(db, du, lax.rem(me_u + nsub - du, nsub)).wait_recv()
        place(own.at[db], base + db * rows, nsub)
    spec = spectrum(x32[...], dft_v)
    power = sum(g * g for g in groups(spec))
    sums = [power[c : c + prow] for c in range(0, base, prow)]
    part_sum = functools.reduce(jnp.add, sums)
    sums = [power[c : c + rows] for c in range(base, base + nblk * rows, rows)]
    own_sum = functools.reduce(jnp.add, sums)
    high, low = split(jnp.concatenate([part_sum, own_sum], axis=0))
    total = mxu(jnp.concatenate([high, low], axis=0), band_ones())
    level = (total[: prow + rows] + total[prow + rows :]) * (1.0 / (BAND * nblk))
    factor = jnp.tile(lax.rsqrt(level + eps) * vcol[...], (1, 8))
    row_id = lax.broadcasted_iota(jnp.int32, (prow, 1), 0) // wide
    partner = []
    for db in range(nblk):
        w = jnp.zeros((prow, 1), jnp.float32)
        seg = lax.rem(me_b + nblk - db, nblk)
        for n in range(nblk):
            w = jnp.where(row_id == n, select[0, n, seg].astype(jnp.float32), w)
        partner.append(rounded(spec[db * prow : (db + 1) * prow] * factor[:prow]) * w)

    owns = []
    for db in range(nblk):
        first = base + db * rows
        owns.append(rounded(spec[first : first + rows] * factor[prow:]))
    parts = []
    for i in range(rows):
        real, imag = 0.0, 0.0
        for db in range(nblk):
            br, bi = partner[db][:, :BINS], partner[db][:, BINS:]
            ar, ai = owns[db][i : i + 1, :BINS], owns[db][i : i + 1, BINS:]
            real = real + (ar * br + ai * bi)
            imag = imag + (ai * br - ar * bi)
        parts.append(jnp.concatenate([real, imag], axis=1))
    out[...] = lags_of(jnp.concatenate(parts, axis=0), lag_v)
    for copy in sent:
        copy.wait_send()


def fused(nblk, nsub, raw, valid, select):
    wide = raw.shape[1]
    rows, prow = wide * nsub, wide * nblk
    tables = (
        jnp.asarray(dft_split()),
        jnp.asarray(lag_split(1.0 / math.sqrt(BINS * nblk))),
    )
    hbm = pl.BlockSpec(memory_space=pltpu.HBM)
    result = pl.pallas_call(
        functools.partial(kernel, nblk, nsub, wide),
        out_shape=jax.ShapeDtypeStruct((rows * prow, LAGS), jnp.float32),
        in_specs=[hbm] * 5,
        out_specs=pl.BlockSpec(memory_space=pltpu.VMEM),
        scratch_shapes=[
            pltpu.SMEM(select.shape, jnp.int32),
            pltpu.VMEM((nblk, nblk, wide, SEG_LEN), jnp.bfloat16),
            pltpu.VMEM((nblk, nsub, wide, SEG_LEN), jnp.bfloat16),
            pltpu.VMEM((nblk, 1, wide), jnp.int32),
            pltpu.VMEM((nsub, 1, wide), jnp.int32),
            pltpu.VMEM((nblk * (rows + prow), SEG_LEN), jnp.float32),
            pltpu.VMEM((rows + prow, 128), jnp.float32),
            pltpu.VMEM((2, 3 * QUARTER, BINS), jnp.bfloat16),
            pltpu.VMEM((2, 3 * QUARTER, LAGS), jnp.bfloat16),
            pltpu.SemaphoreType.DMA((nblk,)),
            pltpu.SemaphoreType.DMA((nblk,)),
            pltpu.SemaphoreType.DMA((nblk + nsub,)),
            pltpu.SemaphoreType.DMA((nblk + nsub,)),
            pltpu.SemaphoreType.DMA((nblk, nsub)),
            pltpu.SemaphoreType.DMA((nblk, nsub)),
            pltpu.SemaphoreType.DMA((5,)),
            pltpu.SemaphoreType.DMA((2,)),
        ],
        compiler_params=pltpu.CompilerParams(
            collective_id=0, has_side_effects=True, vmem_limit_bytes=32 * 2**20
        ),
    )(*(pltpu.with_memory_space_constraint(a, pltpu.HBM) for a in (raw, valid, select) + tables))
    return result.reshape(rows, nblk, wide, LAGS)


def dft_tables(length, bins):
    times = jnp.arange(length, dtype=jnp.int32)[:, None]
    freqs = jnp.arange(bins, dtype=jnp.int32)[None, :]
    angle = (times * freqs % length).astype(jnp.float32) * (2.0 * math.pi / length)
    return (jnp.cos(angle), -jnp.sin(angle))


def whiten(records, valid, seg_len, band):
    chans = records.shape[0] * records.shape[1]
    frames = records.astype(jnp.float32).reshape(chans, -1, seg_len)
    segs = frames.shape[1]
    bins = seg_len // 2
    cos_tab, sin_tab = dft_tables(seg_len, bins)
    real = jnp.einsum("cst,tf->csf", frames, cos_tab, precision=lax.Precision.HIGHEST)
    imag = jnp.einsum("cst,tf->csf", frames, sin_tab, precision=lax.Precision.HIGHEST)
    bands = bins // band
    power = (real * real + imag * imag).reshape(chans, segs, bands, band)
    level = jnp.mean(power, axis=(1, 3))
    factor = valid.reshape(chans, 1).astype(jnp.float32) / jnp.sqrt(level + eps)
    factor = factor[:, None, :, None]
    real = (real.reshape(chans, segs, bands, band) * factor).reshape(chans, segs, bins)
    imag = (imag.reshape(chans, segs, bands, band) * factor).reshape(chans, segs, bins)
    return jnp.stack([real, imag], axis=2).astype(jnp.bfloat16)


def lag_table(bins, lags, seg_len, scale):
    freqs = jnp.arange(bins, dtype=jnp.int32)[:, None]
    shifts = jnp.arange(lags, dtype=jnp.int32)[None, :] - lags // 2
    angle = (freqs * shifts % seg_len).astype(jnp.float32) * (2.0 * math.pi / seg_len)
    weight = jnp.where(freqs == 0, 1.0, 2.0).astype(jnp.float32) * scale
    return jnp.stack([weight * jnp.cos(angle), -weight * jnp.sin(angle)])


def pair_terms(own, weight_rows, piece):
    masked = piece * weight_rows.astype(jnp.bfloat16)[:, None, :, None, None]
    prod = jnp.einsum("isaf,njsbf->injabf", own, masked, preferred_element_type=jnp.float32)
    real = prod[:, :, :, 0, 0] + prod[:, :, :, 1, 1]
    imag = prod[:, :, :, 1, 0] - prod[:, :, :, 0, 1]
    return jnp.stack([real, imag], axis=3)


def by_collectives(raw, valid, select):
    regrouped = lax.all_to_all(raw, "blk", split_axis=0, concat_axis=2, tiled=True)
    spectra = whiten(regrouped, valid, SEG_LEN, BAND)
    segs = spectra.shape[1]
    table = lag_table(BINS, LAGS, SEG_LEN, 1.0 / math.sqrt(BINS * segs))
    block = lax.all_gather(spectra, "sub", axis=0, tiled=True)
    stacked = pair_terms(
        block, select[0], lax.all_gather(spectra[None], "blk", axis=0, tiled=True)
    )
    return jnp.einsum("injrf,rfl->injl", stacked, table, precision=lax.Precision.HIGHEST)


def solution(mesh):
    nblk, nsub = mesh.shape["blk"], mesh.shape["sub"]

    def per_device(raw, valid, select):
        fits = raw.shape[2] == SEG_LEN and raw.shape[0] == nblk and nblk * nsub <= 16
        if fits:
            return fused(nblk, nsub, raw, valid, select)
        return by_collectives(raw, valid, select)

    return jax.shard_map(
        per_device,
        mesh=mesh,
        in_specs=(
            P("cable", "sub", "blk"),
            P(("cable", "blk"), "sub"),
            P(("cable", "blk"), None, None),
        ),
        out_specs=P(("cable", "blk"), None, "sub", None),
        check_vma=False,
    )
```

```python
import functools
import math

import jax
import jax.numpy as jnp
import numpy as np
from jax import lax
from jax.experimental import pallas as pl
from jax.experimental.pallas import tpu as pltpu
from jax.sharding import PartitionSpec as P

SEG_LEN = 1024
BAND = 64
LAGS = 512
BINS = SEG_LEN // 2
QUARTER = SEG_LEN // 4
GROUP = BINS // 4

eps = 1e-06
MESH = pl.DeviceIdType.MESH


def split_table(table):
    high = table.astype(np.float32).astype(jnp.bfloat16)
    low = (table - high.astype(np.float64)).astype(np.float32).astype(jnp.bfloat16)
    return np.stack([high, low])


def waves(freqs, times):
    angle = (freqs * times % SEG_LEN) * (2.0 * math.pi / SEG_LEN)
    return np.cos(angle), -np.sin(angle)


def bins_of(*classes):
    return np.concatenate([np.arange(r, BINS, 4) for r in classes])


def dft_split():
    def table(length, *classes):
        freqs = bins_of(*classes)[None, :]
        return np.concatenate(waves(freqs, np.arange(length)[:, None]), axis=1)

    even = np.concatenate([table(QUARTER, 0), table(QUARTER, 2)], axis=1)
    return split_table(np.concatenate([even, table(2 * QUARTER, 1, 3)], axis=0))


def lag_split(scale):
    def table(count, *classes):
        freqs = bins_of(*classes)[:, None]
        weight = np.where(freqs == 0, 1.0, 2.0) * scale
        shifts = np.arange(count)[None, :] - LAGS // 2
        return np.concatenate([weight * w for w in waves(freqs, shifts)], axis=0)

    even = np.concatenate([table(LAGS // 2, 0), table(LAGS // 2, 2)], axis=1)
    return split_table(np.concatenate([even, table(LAGS, 1, 3)], axis=0))


def band_ones():
    width = BAND // 4
    first = lax.broadcasted_iota(jnp.int32, (GROUP, GROUP), 0) // width
    second = lax.broadcasted_iota(jnp.int32, (GROUP, GROUP), 1) // width
    return jnp.where(first == second, 1.0, 0.0).astype(jnp.bfloat16)


def split(x):
    high = x.astype(jnp.bfloat16)
    low = (x - high.astype(jnp.float32)).astype(jnp.bfloat16)
    return high, low


def mxu(a, b):
    return jnp.dot(a, b, preferred_element_type=jnp.float32)


def rounded(v):
    return v.astype(jnp.bfloat16).astype(jnp.float32)


def groups(v):
    return [v[:, c : c + GROUP] for c in range(0, v.shape[1], GROUP)]


def wide_mxu(v, table, rows, cols):
    high, low = split(v)
    count = v.shape[0]
    first = mxu(jnp.concatenate([high, low], axis=0), table[0, rows, cols])
    return first[:count] + first[count:] + mxu(high, table[1, rows, cols])


EVEN, ODD = slice(0, QUARTER), slice(QUARTER, 3 * QUARTER)
LEFT, RIGHT, ALL = slice(0, QUARTER), slice(QUARTER, 2 * QUARTER), slice(None)


def spectrum(x, table):
    q = [x[:, c : c + QUARTER] for c in range(0, SEG_LEN, QUARTER)]
    plus, cross = q[0] + q[2], q[1] + q[3]
    zero = wide_mxu(plus + cross, table, EVEN, LEFT)
    two = wide_mxu(plus - cross, table, EVEN, RIGHT)
    odd = wide_mxu(
        jnp.concatenate([q[0] - q[2], q[1] - q[3]], axis=1), table, ODD, ALL)
    real = [zero[:, :GROUP], two[:, :GROUP], odd[:, : 2 * GROUP]]
    imag = [zero[:, GROUP:], two[:, GROUP:], odd[:, 2 * GROUP :]]
    return jnp.concatenate(real + imag, axis=1)


def lags_of(v, table):
    g = groups(v)
    zero = wide_mxu(jnp.concatenate([g[0], g[4]], axis=1), table, EVEN, LEFT)
    two = wide_mxu(jnp.concatenate([g[1], g[5]], axis=1), table, EVEN, RIGHT)
    odd = wide_mxu(
        jnp.concatenate([g[2], g[3], g[6], g[7]], axis=1), table, ODD, ALL)
    return jnp.concatenate([zero + two, zero - two], axis=1) + odd


def kernel(
    nblk, nsub, wide,
    raw, valid, choose, dft, lag, out,
    select, part, own, vpart, vown, x32, vcol, dft_v, lag_v,
    send, recv, vsend, vrecv, fsend, frecv, local, tabs,
):
    me_b, me_u = lax.axis_index("blk"), lax.axis_index("sub")
    rows = wide * nsub
    prow = wide * nblk
    blks, subs = range(1, nblk), range(1, nsub)

    def at_blk(db):
        return {"blk": lax.rem(me_b + db, nblk)}

    def at_sub(du):
        return {"sub": lax.rem(me_u + du, nsub)}

    tab_copies = [
        pltpu.make_async_copy(dft, dft_v, tabs.at[0]),
        pltpu.make_async_copy(lag, lag_v, tabs.at[1]),
    ]
    mine = [
        pltpu.make_async_copy(raw, part.at[0], local.at[0]),
        pltpu.make_async_copy(valid, vpart.at[me_b], local.at[1]),
        pltpu.make_async_copy(valid, vown.at[me_u], local.at[2]),
        pltpu.make_async_copy(choose, select, local.at[3]),
        pltpu.make_async_copy(raw.at[me_b], own.at[0, me_u], local.at[4]),
    ]

    barrier = pltpu.get_barrier_semaphore()
    order = list(blks)
    others = [(db, du) for db in range(nblk) for du in range(nsub) if db or du]
    for db, du in others:
        pl.semaphore_signal(
            barrier, inc=1, device_id={**at_blk(db), **at_sub(du)}, device_id_type=MESH)
    for copy in mine:
        copy.start()
    pl.semaphore_wait(barrier, len(others))

    def samples(db):
        return pltpu.make_async_remote_copy(
            part.at[0], part.at[db], send.at[db], recv.at[db],
            device_id=at_blk(db), device_id_type=MESH)

    def valid_blk(db, at_b):
        return pltpu.make_async_remote_copy(
            valid, vpart.at[at_b], vsend.at[db], vrecv.at[db],
            device_id=at_blk(db), device_id_type=MESH)

    def valid_sub(du, at_u):
        return pltpu.make_async_remote_copy(
            valid, vown.at[at_u], vsend.at[nblk + du], vrecv.at[nblk + du],
            device_id=at_sub(du), device_id_type=MESH)

    def block(db, du, at_u):
        there = at_blk(db)
        return pltpu.make_async_remote_copy(
            part.at[0, there["blk"]], own.at[db, at_u], fsend.at[db, du], frecv.at[db, du],
            device_id={**there, **at_sub(du)}, device_id_type=MESH)

    for copy in mine:
        copy.wait()
    sent = [samples(db) for db in order]
    sent += [valid_blk(db, me_b) for db in order]
    sent += [valid_sub(du, me_u) for du in subs]
    sent += [block(db, du, me_u) for db in order for du in subs]
    sent += [block(0, du, me_u) for du in subs]
    for copy in sent + tab_copies:
        copy.start()

    def place(ref, base, count):
        for c in range(count):
            x32[pl.ds(base + c * wide, wide), :] = ref[c].astype(jnp.float32)

    base = nblk * prow
    for db in blks:
        valid_blk(db, lax.rem(me_b + nblk - db, nblk)).wait_recv()
    for du in subs:
        valid_sub(du, lax.rem(me_u + nsub - du, nsub)).wait_recv()
    for n in range(nblk):
        for k in range(wide):
            vcol[pl.ds(n * wide + k, 1), :] = jnp.broadcast_to(
                vpart[n][:, k : k + 1].astype(jnp.float32), (1, 128))
    for u in range(nsub):
        for k in range(wide):
            vcol[pl.ds(prow + u * wide + k, 1), :] = jnp.broadcast_to(
                vown[u][:, k : k + 1].astype(jnp.float32), (1, 128))
    place(part.at[0], 0, nblk)
    moved = []
    for db in order:
        samples(db).wait_recv()
        keep = pltpu.make_async_copy(
            part.at[db, me_b], own.at[db, me_u], fsend.at[db, 0])
        keep.start()
        moved.append(keep)
        place(part.at[db], db * prow, nblk)

    tab_copies[0].wait()
    tab_copies[1].wait()
    for copy in moved:
        copy.wait()
    for db in [0] + order:
        for du in subs:
            block(db, du, lax.rem(me_u + nsub - du, nsub)).wait_recv()
        place(own.at[db], base + db * rows, nsub)
    spec = spectrum(x32[...], dft_v)
    power = sum(g * g for g in groups(spec))
    sums = [power[c : c + prow] for c in range(0, base, prow)]
    part_sum = functools.reduce(jnp.add, sums)
    sums = [power[c : c + rows] for c in range(base, base + nblk * rows, rows)]
    own_sum = functools.reduce(jnp.add, sums)
    high, low = split(jnp.concatenate([part_sum, own_sum], axis=0))
    total = mxu(jnp.concatenate([high, low], axis=0), band_ones())
    level = (total[: prow + rows] + total[prow + rows :]) * (1.0 / (BAND * nblk))
    factor = jnp.tile(lax.rsqrt(level + eps) * vcol[...], (1, 8))
    row_id = lax.broadcasted_iota(jnp.int32, (prow, 1), 0) // wide
    partner = []
    for db in range(nblk):
        w = jnp.zeros((prow, 1), jnp.float32)
        seg = lax.rem(me_b + nblk - db, nblk)
        for n in range(nblk):
            w = jnp.where(row_id == n, select[0, n, seg].astype(jnp.float32), w)
        partner.append(rounded(spec[db * prow : (db + 1) * prow] * factor[:prow]) * w)

    owns = []
    for db in range(nblk):
        first = base + db * rows
        owns.append(rounded(spec[first : first + rows] * factor[prow:]))
    parts = []
    for i in range(rows):
        real, imag = 0.0, 0.0
        for db in range(nblk):
            br, bi = partner[db][:, :BINS], partner[db][:, BINS:]
            ar, ai = owns[db][i : i + 1, :BINS], owns[db][i : i + 1, BINS:]
            real = real + (ar * br + ai * bi)
            imag = imag + (ai * br - ar * bi)
        parts.append(jnp.concatenate([real, imag], axis=1))
    out[...] = lags_of(jnp.concatenate(parts, axis=0), lag_v)
    for copy in sent:
        copy.wait_send()


def fused(nblk, nsub, raw, valid, select):
    wide = raw.shape[1]
    rows, prow = wide * nsub, wide * nblk
    tables = (
        jnp.asarray(dft_split()),
        jnp.asarray(lag_split(1.0 / math.sqrt(BINS * nblk))),
    )
    hbm = pl.BlockSpec(memory_space=pltpu.HBM)
    result = pl.pallas_call(
        functools.partial(kernel, nblk, nsub, wide),
        out_shape=jax.ShapeDtypeStruct((rows * prow, LAGS), jnp.float32),
        in_specs=[hbm] * 5,
        out_specs=pl.BlockSpec(memory_space=pltpu.VMEM),
        scratch_shapes=[
            pltpu.SMEM(select.shape, jnp.int32),
            pltpu.VMEM((nblk, nblk, wide, SEG_LEN), jnp.bfloat16),
            pltpu.VMEM((nblk, nsub, wide, SEG_LEN), jnp.bfloat16),
            pltpu.VMEM((nblk, 1, wide), jnp.int32),
            pltpu.VMEM((nsub, 1, wide), jnp.int32),
            pltpu.VMEM((nblk * (rows + prow), SEG_LEN), jnp.float32),
            pltpu.VMEM((rows + prow, 128), jnp.float32),
            pltpu.VMEM((2, 3 * QUARTER, BINS), jnp.bfloat16),
            pltpu.VMEM((2, 3 * QUARTER, LAGS), jnp.bfloat16),
            pltpu.SemaphoreType.DMA((nblk,)),
            pltpu.SemaphoreType.DMA((nblk,)),
            pltpu.SemaphoreType.DMA((nblk + nsub,)),
            pltpu.SemaphoreType.DMA((nblk + nsub,)),
            pltpu.SemaphoreType.DMA((nblk, nsub)),
            pltpu.SemaphoreType.DMA((nblk, nsub)),
            pltpu.SemaphoreType.DMA((5,)),
            pltpu.SemaphoreType.DMA((2,)),
        ],
        compiler_params=pltpu.CompilerParams(
            collective_id=0, has_side_effects=True, vmem_limit_bytes=32 * 2**20
        ),
    )(*(pltpu.with_memory_space_constraint(a, pltpu.HBM) for a in (raw, valid, select) + tables))
    return result.reshape(rows, nblk, wide, LAGS)


def dft_tables(length, bins):
    times = jnp.arange(length, dtype=jnp.int32)[:, None]
    freqs = jnp.arange(bins, dtype=jnp.int32)[None, :]
    angle = (times * freqs % length).astype(jnp.float32) * (2.0 * math.pi / length)
    return (jnp.cos(angle), -jnp.sin(angle))


def whiten(records, valid, seg_len, band):
    chans = records.shape[0] * records.shape[1]
    frames = records.astype(jnp.float32).reshape(chans, -1, seg_len)
    segs = frames.shape[1]
    bins = seg_len // 2
    cos_tab, sin_tab = dft_tables(seg_len, bins)
    real = jnp.einsum("cst,tf->csf", frames, cos_tab, precision=lax.Precision.HIGHEST)
    imag = jnp.einsum("cst,tf->csf", frames, sin_tab, precision=lax.Precision.HIGHEST)
    bands = bins // band
    power = (real * real + imag * imag).reshape(chans, segs, bands, band)
    level = jnp.mean(power, axis=(1, 3))
    factor = valid.reshape(chans, 1).astype(jnp.float32) / jnp.sqrt(level + eps)
    factor = factor[:, None, :, None]
    real = (real.reshape(chans, segs, bands, band) * factor).reshape(chans, segs, bins)
    imag = (imag.reshape(chans, segs, bands, band) * factor).reshape(chans, segs, bins)
    return jnp.stack([real, imag], axis=2).astype(jnp.bfloat16)


def lag_table(bins, lags, seg_len, scale):
    freqs = jnp.arange(bins, dtype=jnp.int32)[:, None]
    shifts = jnp.arange(lags, dtype=jnp.int32)[None, :] - lags // 2
    angle = (freqs * shifts % seg_len).astype(jnp.float32) * (2.0 * math.pi / seg_len)
    weight = jnp.where(freqs == 0, 1.0, 2.0).astype(jnp.float32) * scale
    return jnp.stack([weight * jnp.cos(angle), -weight * jnp.sin(angle)])


def pair_terms(own, weight_rows, piece):
    masked = piece * weight_rows.astype(jnp.bfloat16)[:, None, :, None, None]
    prod = jnp.einsum("isaf,njsbf->injabf", own, masked, preferred_element_type=jnp.float32)
    real = prod[:, :, :, 0, 0] + prod[:, :, :, 1, 1]
    imag = prod[:, :, :, 1, 0] - prod[:, :, :, 0, 1]
    return jnp.stack([real, imag], axis=3)


def by_collectives(raw, valid, select):
    regrouped = lax.all_to_all(raw, "blk", split_axis=0, concat_axis=2, tiled=True)
    spectra = whiten(regrouped, valid, SEG_LEN, BAND)
    segs = spectra.shape[1]
    table = lag_table(BINS, LAGS, SEG_LEN, 1.0 / math.sqrt(BINS * segs))
    block = lax.all_gather(spectra, "sub", axis=0, tiled=True)
    stacked = pair_terms(
        block, select[0], lax.all_gather(spectra[None], "blk", axis=0, tiled=True)
    )
    return jnp.einsum("injrf,rfl->injl", stacked, table, precision=lax.Precision.HIGHEST)


def solution(mesh):
    nblk, nsub = mesh.shape["blk"], mesh.shape["sub"]

    def per_device(raw, valid, select):
        fits = raw.shape[2] == SEG_LEN and raw.shape[0] == nblk and nblk * nsub <= 16
        if fits:
            return fused(nblk, nsub, raw, valid, select)
        return by_collectives(raw, valid, select)

    return jax.shard_map(
        per_device,
        mesh=mesh,
        in_specs=(
            P("cable", "sub", "blk"),
            P(("cable", "blk"), "sub"),
            P(("cable", "blk"), None, None),
        ),
        out_specs=P(("cable", "blk"), None, "sub", None),
        check_vma=False,
    )
```
